512 devices in a mesh: row: 128 (over y, z, core), col: 4 (over x).
Axes of the slice: x: 4, y: 8, z: 8, core: 2. Of those that a mesh axis runs over, the one named last changes fastest.
Arguments:
- rhs: float32 [2, 128, 1024, 128], P(None, 'row'), may hold values from -6 to 6
- diag_inv: bfloat16 [4, 1024, 1024], P(None, 'row'), as said below
- blocks: bfloat16 [1, 4, 128, 1, 1024, 1024], P(None, 'col', 'row'), may hold values from -0.09375 to 0.09375
- block_rows: int32 [1, 4, 128, 1], P(None, 'col', 'row'), may hold values from 0 to 1, as said below
- counts: int32 [1, 4, 128], P(None, 'col', 'row'), may hold values from 0 to 1, as said below
Outputs:
- solved: float32 [1, 4, 1024, 128], P(None, 'col')
- remainder: float32 [2, 128, 1024, 128], P(None, 'row')
The draws below stay inside these ranges and needn't reach their ends.
Inputs may be any that keep to these rules, and one draw needn't show every extreme that they name: `diag_inv`: lower triangular. `block_rows`: the 1 entries of one list are different; for row indices r below 4, slot 0 lists local block row 0. `counts`: 1 is reached in every draw; for row indices r below 4 the count is 1.
All inputs are finite; a program needn't handle non-finite values.
Results may differ from the reference program's by a relative error of at most 0.0041.
Values may be sent and summed in bfloat16 or wider, within the bound.
A program may use at most 64 MiB of HBM per device.

```python
import jax
import jax.numpy as jnp
from jax import lax

BS = 1024
RHS = 128
RB_DEV = 2
NZ_DEV = 1
KC = 4
KJ = 1
N_ROW = 128
N_COL = 4


def draw_diag_inv(key, part):
    key = jax.random.fold_in(key, 3)
    first, second = jax.random.split(key)
    off = jax.random.normal(first, (KC, BS, BS), jnp.float32) / jnp.sqrt(jnp.float32(BS))
    scales = jnp.exp(jax.random.uniform(second, (KC, BS), jnp.float32, jnp.log(0.5), jnp.log(1.5)))
    lower = jnp.tril(off, -1)
    eye = jnp.eye(BS, dtype=jnp.float32)
    return (lower + eye[None] * scales[:, :, None]).astype(jnp.bfloat16)


def draw_block_rows(key, part):
    key = jax.random.fold_in(key, 1)
    scores = jax.random.randint(key, (KJ, N_COL, N_ROW, RB_DEV), 0, 1 << 20) * RB_DEV
    scores = scores + jnp.arange(RB_DEV, dtype=jnp.int32)
    ranks = jnp.arange(N_ROW, dtype=jnp.int32)[:, None]
    locals_ids = jnp.arange(RB_DEV, dtype=jnp.int32)[None, :]
    forced = ((ranks < KC) & (locals_ids == 0)).astype(jnp.int32)
    scores = scores - forced * (1 << 23)
    order = jnp.argsort(scores, axis=-1, stable=True)
    return order[..., :NZ_DEV].astype(jnp.int32)


def draw_counts(key, part):
    key = jax.random.fold_in(key, 2)
    first, second = jax.random.split(key)
    base = jax.random.randint(first, (KJ * N_COL * N_ROW,), 0, NZ_DEV + 1)
    pick = jax.random.randint(second, (), 0, KJ * N_COL * N_ROW)
    spots = jnp.arange(KJ * N_COL * N_ROW, dtype=jnp.int32)
    base = jnp.where(spots == pick, NZ_DEV, base)
    ranks = spots % N_ROW
    base = jnp.where(ranks < KC, NZ_DEV, base)
    return base.reshape(KJ, N_COL, N_ROW).astype(jnp.int32)


def shard_levels(rng, shape, pieces, smallest, largest):
    def one(dim, shards_of):
        heights = jax.random.uniform(jax.random.fold_in(jax.random.fold_in(rng, 6), dim), (shards_of,), jnp.float32, smallest / len(pieces), largest / len(pieces))
        return jnp.repeat(jnp.exp(heights), shape[dim] // shards_of).reshape((-1,) + (1,) * (len(shape) - dim - 1))

    gain = one(*pieces[0])
    for cut in pieces[1:]:
        gain = gain * one(*cut)
    return gain


def bell_draw(key, extent, deviation, reach, cuts=(), kind=jnp.bfloat16):
    drawn = deviation * jax.random.normal(key, extent, jnp.float32)
    if cuts:
        drawn = drawn * shard_levels(key, extent, cuts, -0.22, 0.18)
    return jnp.clip(drawn, -reach, reach).astype(kind)


def setup_inputs(seed: int = 0) -> dict:
    arg_keys = jax.random.split(jax.random.key(seed), 6)
    rhs = bell_draw(arg_keys[0], (RB_DEV, N_ROW, BS, RHS), 1.0, 6.0, ((1, 128),), jnp.float32)
    diag_inv = draw_diag_inv(jax.random.fold_in(arg_keys[5], 71), 0)
    blocks = bell_draw(arg_keys[2], (KJ, N_COL, N_ROW, NZ_DEV, BS, BS), (4 * BS) ** -0.5, 0.09375, ((1, 4), (2, 128)))
    block_rows = draw_block_rows(jax.random.fold_in(arg_keys[5], 71), 0)
    counts = draw_counts(jax.random.fold_in(arg_keys[5], 71), 0)
    return dict(rhs=rhs, diag_inv=diag_inv, blocks=blocks, block_rows=block_rows, counts=counts)


def reference(rhs, diag_inv, blocks, block_rows, counts):
    acc = rhs.reshape(RB_DEV * N_ROW, BS, RHS)
    results = []
    ranks = jnp.arange(N_ROW, dtype=jnp.int32)
    slots = jnp.arange(NZ_DEV, dtype=jnp.int32)
    for k in range(KC):
        j = k // N_COL
        c = k % N_COL
        pivot = acc[k].astype(jnp.bfloat16)
        sol = jnp.dot(diag_inv[k], pivot, preferred_element_type=jnp.float32)
        results.append(sol)
        quant = sol.astype(jnp.bfloat16).astype(jnp.float32)
        rows = block_rows[j, c]
        glob = rows * N_ROW + ranks[:, None]
        valid = (slots[None, :] < counts[j, c][:, None]) & (glob > k)
        contrib = jnp.einsum("rsab,bn->rsan", blocks[j, c].astype(jnp.float32), quant, precision=lax.Precision.HIGHEST)
        contrib = jnp.where(valid[:, :, None, None], contrib, jnp.float32(0.0))
        acc = acc.at[glob.reshape(-1)].add(-contrib.reshape(N_ROW * NZ_DEV, BS, RHS))
    solved = jnp.stack(results).reshape(KJ, N_COL, BS, RHS)
    return solved, acc.reshape(RB_DEV, N_ROW, BS, RHS)
```

```python
import functools

import jax
import jax.numpy as jnp
from jax import lax
from jax.experimental import pallas as pl
from jax.experimental.pallas import tpu as pltpu
from jax.sharding import PartitionSpec as P

MESH = pl.DeviceIdType.MESH
F32 = jnp.float32
BF16 = jnp.bfloat16
NY, NZ, NX = 8, 8, 4
BS, RHS = 1024, 128
PIECE = BS // 16


def remote(src, dst, ss, rs, row, col):
    return pltpu.make_async_remote_copy(
        src_ref=src, dst_ref=dst, send_sem=ss, recv_sem=rs,
        device_id={"row": row, "col": col}, device_id_type=MESH,
    )


def matmul(a_ref, b_ref, rows, store, tile=256):
    b = b_ref[...]
    if b.ndim == 3:
        b = b.reshape(BS, RHS)

    def body(i, carry):
        at = pl.ds(pl.multiple_of(i * tile, tile), tile)
        store(at, jnp.dot(a_ref[at, :], b, preferred_element_type=F32))
        return carry

    lax.fori_loop(0, rows // tile, body, 0)


def repack(src, dst, rows):
    def body(i, carry):
        part = src[pl.ds(i * 16, 16)].astype(F32).reshape(128, BS).astype(BF16)
        dst[pl.ds(pl.multiple_of(i * 128, 128), 128), :] = part
        return carry

    lax.fori_loop(0, rows // 128, body, 0)


def kernel(brow_ref, count_ref, rhs_hbm, diag_hbm, blk_hbm, solved_ref, rem_ref,
           rhs, blk, dq, dk, dm, acc, piv, qc, qn, qb, con, wts,
           loc, dsend, drecv, qsend, qrecv, p1send, prec, p2send, p3send, p3rec, p4send, p4rec,
           xsend, xrec, wsend, wrec):
    r = lax.axis_index("row")
    c = lax.axis_index("col")
    core = r % 2
    z = (r // 2) % NZ
    y = r // (2 * NZ)
    is_root = (c < 3) & (r == c + 1)
    support = ((c == 0) & ((r == 2) | (r == 3))) | ((c == 1) & (r == 3))
    early = is_root | support
    in_quarter = (r // 32) == c

    def at(yy, zz, kk):
        return (yy * NZ + zz) * 2 + kk

    barrier = pltpu.get_barrier_semaphore()

    def signal(row, col):
        pl.semaphore_signal(barrier, inc=1, device_id={"row": row, "col": col}, device_id_type=MESH)

    @pl.when(is_root)
    def _():
        def body(i, carry):
            signal((r + i) % 128, c)
            return carry

        lax.fori_loop(1, 128, body, 0)

    @pl.when(r == 0)
    def _():
        def body(i, carry):
            @pl.when((c > 0) | (i > 0))
            def _():
                signal(32 * c + i, c)
            return carry

        lax.fori_loop(0, 32, body, 0)

    @pl.when((c == 0) & (r >= 1) & (r <= 3))
    def _():
        for cc in range(4):
            signal(0, cc)

    @pl.when((c == 1) & (r == 2))
    def _():
        signal(1, 0)

    @pl.when((c == 2) & (r == 3))
    def _():
        signal(2, 1)

    @pl.when((c == 3) & (y == 0))
    def _():
        signal(3, 2)

    for d in range(1, 8):
        signal(at((y + d) % NY, z, core), c)
        signal(at(y, (z + d) % NZ, core), c)
        signal(at(y, (z + d) % NZ, 1 - core), c)
    signal(at(y, z, 1 - core), c)
    for d in range(1, 4):
        signal(r, (c + d) % NX)

    load_rhs = pltpu.make_async_copy(rhs_hbm, rhs, loc.at[0])
    load_blk = pltpu.make_async_copy(blk_hbm, blk, loc.at[1])
    load_rhs.start()
    load_blk.start()

    k_row = brow_ref[0]
    glob = k_row * 128 + r
    valid = (count_ref[0] > 0) & (glob > c)
    for i in range(2):
        w = jnp.where(valid & (k_row == i), F32(1.0), F32(0.0))
        wts[c, i] = jnp.full((8, RHS), w, F32)

    need = 25 + jnp.where((c < 3) & jnp.logical_not(is_root), 1, 0)
    need = need + jnp.where(in_quarter & (r > 0), 1, 0)
    need = need + jnp.where(r == 0, 3, 0)
    need = need + jnp.where((c < 2) & is_root, 1, 0)
    need = need + jnp.where((c == 2) & is_root, 16, 0)
    pl.semaphore_wait(barrier, need)

    @pl.when(in_quarter & (r > 0))
    def _():
        remote(diag_hbm.at[0], dq.at[r % 32], dsend.at[0], drecv.at[0], 0, c).start()

    @pl.when(in_quarter & (r == 0))
    def _():
        pltpu.make_async_copy(diag_hbm.at[0], dq.at[0], drecv.at[0]).start()

    @pl.when((c < 3) & jnp.logical_not(is_root))
    def _():
        remote(diag_hbm.at[c + 1], dk.at[r], dsend.at[1], drecv.at[1], c + 1, c).start()

    @pl.when(is_root)
    def _():
        pltpu.make_async_copy(diag_hbm.at[c + 1], dk.at[r], drecv.at[1]).start()

    for d in range(1, 4):
        remote(wts.at[c], wts.at[c], wsend.at[d - 1], wrec.at[c], r, (c + d) % NX).start()

    load_rhs.wait()
    load_blk.wait()

    def store_con(sl, v):
        con[c, sl, :] = v.astype(BF16)

    def send_con():
        for d in range(1, 4):
            remote(con.at[c], con.at[c], xsend.at[d - 1], xrec.at[c], r, (c + d) % NX).start()

    def wait_con(j):
        pltpu.make_async_copy(con.at[j], con.at[j], xrec.at[j]).wait()

    @pl.when(r == 0)
    def _():
        piv[...] = rhs[0].astype(BF16)
        pltpu.make_async_copy(dq, dq, drecv.at[0]).wait()
        repack(dq, dm, 256)

        def store(sl, v):
            qn[pl.ds(4 * c, 4)] = v.astype(BF16).reshape(4, PIECE, RHS)

        matmul(dm, piv, 256, store)
        for t in range(1, 4):
            part = pl.ds(4 * c, 4)
            remote(qn.at[part], qc.at[part], qsend.at[t - 1], qrecv, t, 0).start()

    @pl.when(is_root)
    def _():
        pltpu.make_async_copy(dk, dk, drecv.at[1]).wait()
        repack(dk, dm, BS)

    @pl.when(early)
    def _():
        pltpu.make_async_copy(qc, qc, qrecv).wait()

    @pl.when((c == 1) & (r == 2))
    def _():
        remote(qc, qc, qsend.at[1], qrecv, 3, 1).start()

    @pl.when(is_root)
    def _():
        def store(sl, v):
            acc[sl, :] = rhs[0, sl, :] - v
            con[c, sl, :] = v.astype(BF16)

        matmul(blk, qc, BS, store)

        def body(j, carry):
            wait_con(j)
            acc[...] = acc[...] - con[j].astype(F32)
            return carry

        lax.fori_loop(0, c, body, 0)
        piv[...] = acc[...].astype(BF16)

        def store_q(sl, v):
            n = v.shape[0] // PIECE
            qn[pl.ds(sl.start // PIECE, n)] = v.astype(BF16).reshape(n, PIECE, RHS)

        matmul(dm, piv, BS, store_q)

    @pl.when(is_root & (c < 2))
    def _():
        remote(qn, qc, qsend.at[0], qrecv, c + 2, c + 1).start()

    @pl.when(is_root & (c == 2))
    def _():
        for p in range(16):
            remote(qn.at[p], qb.at[p], p1send.at[p], prec, (p % 8) * 2 + p // 8, 3).start()

    @pl.when(is_root)
    def _():
        def body(p, carry):
            to = (p % 8) * 2 + p // 8

            @pl.when(to != r)
            def _():
                remote(qc.at[p], qb.at[p], p1send.at[16 + p], prec, to, c).start()

            @pl.when(to == r)
            def _():
                pltpu.make_async_copy(qc.at[p], qb.at[p], prec).start()

            return carry

        lax.fori_loop(0, 16, body, 0)

    @pl.when(support)
    def _():
        matmul(blk, qc, BS, store_con)

    @pl.when(early)
    def _():
        send_con()

    mine = core * 8 + z
    pltpu.make_async_copy(qb.at[mine], qb.at[mine], prec).wait()

    @pl.when(y == 0)
    def _():
        for d in (4, 3, 5, 2, 6, 1, 7):
            remote(qb.at[mine], qb.at[mine], p2send.at[d - 1], prec, at(d, z, core), c).start()

    for d in (4, 3, 5, 2, 6, 1, 7):
        remote(qb.at[mine], qb.at[mine], p3send.at[d - 1], p3rec, at(y, (z + d) % NZ, core), c).start()
    seven = qb.at[pl.ds(0, 7)]
    pltpu.make_async_copy(seven, seven, p3rec).wait()
    half = qb.at[pl.ds(8 * core, 8)]
    remote(half, half, p4send, p4rec, at(y, z, 1 - core), c).start()
    other = qb.at[pl.ds(8 * (1 - core), 8)]
    pltpu.make_async_copy(other, other, p4rec).wait()

    @pl.when(jnp.logical_not(early))
    def _():
        matmul(blk, qb, BS, store_con)
        send_con()

    solved_ref[...] = qb[...].astype(F32).reshape(BS, RHS)

    for j in range(4):
        @pl.when(c != j)
        def _():
            pltpu.make_async_copy(wts.at[j], wts.at[j], wrec.at[j]).wait()

            @pl.when(jnp.logical_not(is_root & (c > j)))
            def _():
                wait_con(j)

        base = rhs if j == 0 else rem_ref
        got = con[j].astype(F32).reshape(BS // 8, 8, RHS)
        for i in range(2):
            step = (got * wts[j, i][None]).reshape(BS, RHS)
            rem_ref[i] = base[i] - step

    @pl.when(in_quarter & (r > 0))
    def _():
        remote(diag_hbm.at[0], dq.at[0], dsend.at[0], drecv.at[0], 0, c).wait_send()

    @pl.when((c < 3) & jnp.logical_not(is_root))
    def _():
        remote(diag_hbm.at[0], dk.at[0], dsend.at[1], drecv.at[1], 0, c).wait_send()

    @pl.when(r == 0)
    def _():
        for t in range(3):
            part = pl.ds(0, 4)
            remote(qn.at[part], qc.at[part], qsend.at[t], qrecv, 1, 0).wait_send()

    @pl.when(is_root & (c < 2))
    def _():
        remote(qn, qc, qsend.at[0], qrecv, 0, 0).wait_send()

    @pl.when((c == 1) & (r == 2))
    def _():
        remote(qc, qc, qsend.at[1], qrecv, 0, 0).wait_send()

    @pl.when(is_root & (c == 2))
    def _():
        for p in range(16):
            remote(qn.at[0], qb.at[0], p1send.at[p], prec, 0, 3).wait_send()

    @pl.when(is_root)
    def _():
        def body(p, carry):
            @pl.when((p % 8) * 2 + p // 8 != r)
            def _():
                remote(qc.at[0], qb.at[0], p1send.at[16 + p], prec, 0, c).wait_send()
            return carry

        lax.fori_loop(0, 16, body, 0)

    @pl.when(y == 0)
    def _():
        for d in range(7):
            remote(qb.at[0], qb.at[0], p2send.at[d], prec, 0, c).wait_send()

    for d in range(7):
        remote(qb.at[0], qb.at[0], p3send.at[d], p3rec, 0, c).wait_send()
    remote(half, half, p4send, p4rec, 0, c).wait_send()
    for d in range(3):
        remote(con.at[0], con.at[0], xsend.at[d], xrec.at[0], 0, c).wait_send()
        remote(wts.at[0], wts.at[0], wsend.at[d], wrec.at[0], 0, c).wait_send()


def on_device(rhs, diag_inv, blocks, block_rows, counts):
    vmem = pl.BlockSpec(memory_space=pltpu.VMEM)
    smem = pl.BlockSpec(memory_space=pltpu.SMEM)
    hbm = pl.BlockSpec(memory_space=pl.ANY)
    dma = pltpu.SemaphoreType.DMA
    solved, rem = pl.pallas_call(
        kernel,
        out_shape=(
            jax.ShapeDtypeStruct((BS, RHS), F32),
            jax.ShapeDtypeStruct((2, BS, RHS), F32),
        ),
        in_specs=[smem, smem, hbm, hbm, hbm],
        out_specs=(vmem, vmem),
        scratch_shapes=[
            pltpu.VMEM((2, BS, RHS), F32),
            pltpu.VMEM((BS, BS), BF16),
            pltpu.VMEM((32, 8, BS), BF16),
            pltpu.VMEM((128, 8, BS), BF16),
            pltpu.VMEM((BS, BS), BF16),
            pltpu.VMEM((BS, RHS), F32),
            pltpu.VMEM((BS, RHS), BF16),
            pltpu.VMEM((16, PIECE, RHS), BF16),
            pltpu.VMEM((16, PIECE, RHS), BF16),
            pltpu.VMEM((16, PIECE, RHS), BF16),
            pltpu.VMEM((4, BS, RHS), BF16),
            pltpu.VMEM((4, 2, 8, RHS), F32),
            dma((2,)), dma((2,)), dma((2,)), dma((3,)), dma,
            dma((32,)), dma, dma((7,)), dma((7,)), dma, dma, dma,
            dma((3,)), dma((4,)), dma((3,)), dma((4,)),
        ],
        compiler_params=pltpu.CompilerParams(
            collective_id=0, has_side_effects=True, vmem_limit_bytes=40 << 20
        ),
    )(
        block_rows.reshape(1), counts.reshape(1), rhs.reshape(2, BS, RHS), diag_inv,
        blocks.reshape(BS, BS),
    )
    return solved.reshape(1, 1, BS, RHS), rem.reshape(2, 1, BS, RHS)


def solution(mesh):
    in_specs = (
        P(None, "row", None, None),
        P(None, "row", None),
        P(None, "col", "row", None, None, None),
        P(None, "col", "row", None),
        P(None, "col", "row"),
    )
    out_specs = (P(None, "col", None, None), P(None, "row", None, None))
    return jax.shard_map(
        on_device, mesh=mesh, in_specs=in_specs, out_specs=out_specs, check_vma=False
    )
```

```python
import functools

import jax
import jax.numpy as jnp
from jax import lax
from jax.experimental import pallas as pl
from jax.experimental.pallas import tpu as pltpu
from jax.sharding import PartitionSpec as P

MESH = pl.DeviceIdType.MESH
F32 = jnp.float32
BF16 = jnp.bfloat16
NY, NZ, NX = 8, 8, 4
BS, RHS = 1024, 128
PIECE = BS // 16


def remote(src, dst, ss, rs, row, col):
    return pltpu.make_async_remote_copy(
        src_ref=src, dst_ref=dst, send_sem=ss, recv_sem=rs,
        device_id={"row": row, "col": col}, device_id_type=MESH,
    )


def kernel(brow_ref, count_ref, rhs_hbm, diag_hbm, blk_hbm, solved_ref, rem_ref,
           rhs, blk, dq, dk, dm, own, rhs_left, piv, qc, qn, qb, con, wts,
           loc, dsend, d0rec, drec, qsend, qrec, fsend, p1send, prec, p2send, p3send, p3rec, p4send, p4rec,
           xsend, xrec, x3send, x3rec, wsend, wrec):
    r = lax.axis_index("row")
    c = lax.axis_index("col")
    core = r % 2
    z = (r // 2) % NZ
    y = r // (2 * NZ)
    is_root = (c < 3) & (r == c + 1)
    support = ((c == 0) & ((r == 2) | (r == 3))) | ((c == 1) & (r == 3))
    early = is_root | support
    in_quarter = (r // 32) == c

    def at(yy, zz, kk):
        return (yy * NZ + zz) * 2 + kk

    drains = []

    def later(cond, *copies):
        def go():
            for copy in copies:
                copy.wait_send()

        drains.append(go if cond is None else lambda: pl.when(cond)(go))

    def finish():
        for drain in drains:
            drain()

    barrier = pltpu.get_barrier_semaphore()

    def signal(row, col):
        pl.semaphore_signal(barrier, inc=1, device_id={"row": row, "col": col}, device_id_type=MESH)

    @pl.when(is_root)
    def _():
        def body(i, carry):
            signal((r + i) % 128, c)
            return carry

        lax.fori_loop(1, 128, body, 0)

    @pl.when(r == 0)
    def _():
        def body(i, carry):
            @pl.when((c > 0) | (i > 0))
            def _():
                signal(32 * c + i, c)
            return carry

        lax.fori_loop(0, 32, body, 0)

    @pl.when((c == 0) & (r >= 1) & (r <= 3))
    def _():
        for cc in range(4):
            signal(0, cc)

    @pl.when((c == 1) & (r == 2))
    def _():
        signal(1, 0)

    @pl.when((c == 2) & (r == 3))
    def _():
        signal(2, 1)

    @pl.when((c == 3) & (y == 0))
    def _():
        signal(3, 2)

    for d in range(1, 8):
        signal(at((y + d) % NY, z, core), c)
        signal(at(y, (z + d) % NZ, core), c)
        signal(at(y, (z + d) % NZ, 1 - core), c)
    signal(at(y, z, 1 - core), c)
    for d in range(1, 4):
        signal(r, (c + d) % NX)

    load_rhs = pltpu.make_async_copy(rhs_hbm, rhs, loc.at[0])
    load_blk = pltpu.make_async_copy(blk_hbm, blk, loc.at[1])
    load_rhs.start()
    load_blk.start()

    k_row = brow_ref[0]
    glob = k_row * 128 + r
    valid = (count_ref[0] > 0) & (glob > c)
    for i in range(2):
        w = jnp.where(valid & (k_row == i), F32(1.0), F32(0.0))
        wts[c, i] = jnp.full((8, RHS), w, F32)

    need = 25 + jnp.where((c < 3) & jnp.logical_not(is_root), 1, 0)
    need = need + jnp.where(in_quarter & (r > 0), 1, 0)
    need = need + jnp.where(r == 0, 3, 0)
    need = need + jnp.where((c < 2) & is_root, 1, 0)
    need = need + jnp.where((c == 2) & is_root, 16, 0)
    pl.semaphore_wait(barrier, need)

    for yy in range(NY):
        width = pl.ds(0, 128 * (yy + 1))

        @pl.when((y == yy) & in_quarter)
        def _():
            @pl.when(r > 0)
            def _():
                remote(diag_hbm.at[0, :, width], dq.at[r % 32, :, width], dsend.at[0], d0rec.at[yy % 2], 0, c).start()

            @pl.when(r == 0)
            def _():
                pltpu.make_async_copy(diag_hbm.at[0, :, width], dq.at[r % 32, :, width], d0rec.at[yy % 2]).start()

        @pl.when((y == yy) & (c < 3))
        def _():
            @pl.when(jnp.logical_not(is_root))
            def _():
                remote(diag_hbm.at[c + 1, :, width], dk.at[r, :, width], dsend.at[1], drec.at[yy], c + 1, c).start()

            @pl.when(is_root)
            def _():
                pltpu.make_async_copy(diag_hbm.at[c + 1, :, width], dk.at[r, :, width], drec.at[yy]).start()

        later((y == yy) & in_quarter & (r > 0),
              remote(diag_hbm.at[0, :, width], dq.at[0, :, width], dsend.at[0], d0rec.at[0], 0, c))
        later((y == yy) & (c < 3) & jnp.logical_not(is_root),
              remote(diag_hbm.at[0, :, width], dk.at[0, :, width], dsend.at[1], drec.at[0], 0, c))

    for d in range(1, 4):
        remote(wts.at[c], wts.at[c], wsend.at[d - 1], wrec.at[c], r, (c + d) % NX).start()

    load_rhs.wait()
    load_blk.wait()

    for d in range(3):
        later(None, remote(wts.at[0], wts.at[0], wsend.at[d], wrec.at[0], 0, c))

    def send_con(d):
        remote(con.at[c], con.at[c], xsend.at[d - 1], xrec.at[c], r, (c + d) % NX).start()

    def wait_con(j):
        pltpu.make_async_copy(con.at[j], con.at[j], xrec.at[j]).wait()

    def squeeze(ref, block, width):
        part = ref[pl.ds(16 * block, 16), :, pl.ds(0, width)]
        return part.astype(F32).reshape(128, width).astype(BF16)

    def put_q(block, v):
        qn[pl.ds(2 * block, 2)] = v.astype(BF16).reshape(2, PIECE, RHS)

    for cc in range(NX):
        @pl.when((r == 0) & (c == cc))
        def _():
            piv[...] = rhs[0].astype(BF16)
            for h in range(2):
                block = 2 * cc + h
                width = 128 * (block + 1)
                sixteen = dq.at[pl.ds(16 * h, 16), :, pl.ds(0, width)]
                pltpu.make_async_copy(sixteen, sixteen, d0rec.at[h]).wait()
                put_q(block, jnp.dot(squeeze(dq, h, width), piv[pl.ds(0, width), :], preferred_element_type=F32))
            part = pl.ds(4 * cc, 4)
            for t in range(1, 4):
                remote(qn.at[part], qc.at[part], qsend.at[t - 1], qrec.at[cc], t, 0).start()

    part0 = pl.ds(0, 4)
    later(r == 0, *[remote(qn.at[part0], qc.at[part0], qsend.at[t], qrec.at[0], 1, 0) for t in range(3)])

    @pl.when(is_root)
    def _():
        for block in range(8):
            width = 128 * (block + 1)
            sixteen = dk.at[pl.ds(16 * block, 16), :, pl.ds(0, width)]
            pltpu.make_async_copy(sixteen, sixteen, drec.at[block]).wait()
            dm[pl.ds(128 * block, 128), pl.ds(0, width)] = squeeze(dk, block, width)

    @pl.when(early)
    def _():
        for g in range(4):
            part = pl.ds(4 * g, 4)
            pltpu.make_async_copy(qc.at[part], qc.at[part], qrec.at[g]).wait()

            @pl.when((c == 1) & (r == 2))
            def _():
                remote(qc.at[part], qc.at[part], fsend.at[g], qrec.at[g], 3, 1).start()

            b = qc[part].reshape(256, RHS)

            def body(i, carry):
                at_rows = pl.ds(pl.multiple_of(i * 256, 256), 256)
                step = jnp.dot(blk[at_rows, pl.ds(256 * g, 256)], b, preferred_element_type=F32)
                own[at_rows, :] = step if g == 0 else own[at_rows, :] + step
                return carry

            lax.fori_loop(0, 4, body, 0)

    @pl.when(is_root)
    def _():
        def body(j, carry):
            wait_con(j)
            rhs_left[...] = rhs_left[...] - con[j].astype(F32)
            return carry

        rhs_left[...] = rhs[0]
        lax.fori_loop(0, c, body, 0)
        piv[...] = (rhs_left[...] - own[...]).astype(BF16)
        for block in range(8):
            width = 128 * (block + 1)
            put_q(block, jnp.dot(dm[pl.ds(128 * block, 128), pl.ds(0, width)], piv[pl.ds(0, width), :],
                                 preferred_element_type=F32))

            @pl.when(c == 2)
            def _():
                for p in (2 * block, 2 * block + 1):
                    remote(qn.at[p], qb.at[p], p1send.at[p], prec, (p % 8) * 2 + p // 8, 3).start()

            if block % 2 == 1:
                @pl.when(c < 2)
                def _():
                    part = pl.ds(2 * block - 2, 4)
                    remote(qn.at[part], qc.at[part], qsend.at[block // 2], qrec.at[block // 2], c + 2, c + 1).start()

    later((c == 1) & (r == 2), *[remote(qc.at[part0], qc.at[part0], fsend.at[g], qrec.at[0], 0, 0) for g in range(4)])
    later(is_root & (c < 2), *[remote(qn.at[part0], qc.at[part0], qsend.at[g], qrec.at[0], 0, 0) for g in range(4)])
    later(is_root & (c == 2), *[remote(qn.at[0], qb.at[0], p1send.at[p], prec, 0, 3) for p in range(16)])

    @pl.when(early)
    def _():
        con[c] = own[...].astype(BF16)

    for d in (1, 2):
        @pl.when(support & (c + d == r - 1))
        def _():
            send_con(d)

    @pl.when(is_root)
    def _():
        def body(p, carry):
            to = (p % 8) * 2 + p // 8

            @pl.when(to != r)
            def _():
                remote(qc.at[p], qb.at[p], p1send.at[16 + p], prec, to, c).start()

            @pl.when(to == r)
            def _():
                pltpu.make_async_copy(qc.at[p], qb.at[p], prec).start()

            return carry

        lax.fori_loop(0, 16, body, 0)

    for p in range(16):
        later(is_root & ((p % 8) * 2 + p // 8 != r), remote(qc.at[0], qb.at[0], p1send.at[16 + p], prec, 0, c))

    mine = core * 8 + z
    pltpu.make_async_copy(qb.at[mine], qb.at[mine], prec).wait()


    @pl.when(y == 0)
    def _():
        for d in (4, 3, 5, 2, 6, 1, 7):
            remote(qb.at[mine], qb.at[mine], p2send.at[d - 1], prec, at(d, z, core), c).start()

    later(y == 0, *[remote(qb.at[0], qb.at[0], p2send.at[d], prec, 0, c) for d in range(7)])
    for d in (4, 3, 5, 2, 6, 1, 7):
        remote(qb.at[mine], qb.at[mine], p3send.at[d - 1], p3rec, at(y, (z + d) % NZ, core), c).start()
    seven = qb.at[pl.ds(0, 7)]
    pltpu.make_async_copy(seven, seven, p3rec).wait()
    later(None, *[remote(qb.at[0], qb.at[0], p3send.at[d], p3rec, 0, c) for d in range(7)])
    half = qb.at[pl.ds(8 * core, 8)]
    remote(half, half, p4send, p4rec, at(y, z, 1 - core), c).start()
    other = qb.at[pl.ds(8 * (1 - core), 8)]
    pltpu.make_async_copy(other, other, p4rec).wait()
    later(None, remote(half, half, p4send, p4rec, 0, c))

    def quarter(j, t):
        return con.at[j, pl.ds(256 * t, 256)]

    def send_quarter(t, col, slot):
        remote(quarter(3, t), quarter(3, t), x3send.at[slot], x3rec.at[t], r, col).start()

    def compute(t):
        at_rows = pl.ds(256 * t, 256)
        b = qb[...].reshape(BS, RHS)
        con[c, at_rows, :] = jnp.dot(blk[at_rows, :], b, preferred_element_type=F32).astype(BF16)

    @pl.when(c == 3)
    def _():
        for t, col in ((0, 0), (2, 2), (1, 0), (3, 2)):
            compute(t)
            send_quarter(t, col, t)
        for t, col in ((2, 0), (0, 2), (3, 0), (1, 2)):
            send_quarter(t, col, 4 + t)

    @pl.when((c < 3) & jnp.logical_not(early))
    def _():
        for t in range(4):
            compute(t)

    for d in (1, 3, 2):
        @pl.when((c < 3) & jnp.logical_not(support & (c + d == r - 1)))
        def _():
            send_con(d)

    later(c < 3, *[remote(con.at[0], con.at[0], xsend.at[d], xrec.at[0], 0, c) for d in range(3)])
    later(c == 3, *[remote(quarter(3, 0), quarter(3, 0), x3send.at[t], x3rec.at[0], 0, c) for t in range(8)])
    later((c == 0) | (c == 2), *[remote(quarter(3, 0), quarter(3, 0), x3send.at[t], x3rec.at[0], 0, c) for t in range(2)])

    solved_ref[...] = qb[...].astype(F32).reshape(BS, RHS)

    for j in range(4):
        @pl.when(c != j)
        def _():
            pltpu.make_async_copy(wts.at[j], wts.at[j], wrec.at[j]).wait()

    def update(j, base, rows):
        got = con[j, rows, :].astype(F32).reshape(rows.size // 8, 8, RHS)
        for i in range(2):
            step = (got * wts[j, i][None]).reshape(rows.size, RHS)
            rem_ref[i, rows, :] = base[i, rows, :] - step

    for j in range(3):
        @pl.when((c != j) & jnp.logical_not(is_root & (c > j)))
        def _():
            wait_con(j)

        update(j, rhs if j == 0 else rem_ref, pl.ds(0, BS))

    for t in (0, 1, 2, 3):
        @pl.when(c == 0)
        def _():
            pltpu.make_async_copy(quarter(3, t), quarter(3, t), x3rec.at[t]).wait()
            if t < 2:
                send_quarter(t, 1, t)

        u = (t + 2) % 4

        @pl.when(c == 2)
        def _():
            pltpu.make_async_copy(quarter(3, u), quarter(3, u), x3rec.at[u]).wait()
            if u >= 2:
                send_quarter(u, 1, u - 2)

        @pl.when(c == 1)
        def _():
            v = (0, 2, 1, 3)[t]
            pltpu.make_async_copy(quarter(3, v), quarter(3, v), x3rec.at[v]).wait()

    update(3, rem_ref, pl.ds(0, BS))

    finish()


def on_device(rhs, diag_inv, blocks, block_rows, counts):
    vmem = pl.BlockSpec(memory_space=pltpu.VMEM)
    smem = pl.BlockSpec(memory_space=pltpu.SMEM)
    hbm = pl.BlockSpec(memory_space=pltpu.HBM)
    dma = pltpu.SemaphoreType.DMA
    solved, rem = pl.pallas_call(
        kernel,
        out_shape=(
            jax.ShapeDtypeStruct((BS, RHS), F32),
            jax.ShapeDtypeStruct((2, BS, RHS), F32),
        ),
        in_specs=[smem, smem, hbm, hbm, hbm],
        out_specs=(vmem, vmem),
        scratch_shapes=[
            pltpu.VMEM((2, BS, RHS), F32),
            pltpu.VMEM((BS, BS), BF16),
            pltpu.VMEM((32, 8, BS), BF16),
            pltpu.VMEM((128, 8, BS), BF16),
            pltpu.VMEM((BS, BS), BF16),
            pltpu.VMEM((BS, RHS), F32),
            pltpu.VMEM((BS, RHS), F32),
            pltpu.VMEM((BS, RHS), BF16),
            pltpu.VMEM((16, PIECE, RHS), BF16),
            pltpu.VMEM((16, PIECE, RHS), BF16),
            pltpu.VMEM((16, PIECE, RHS), BF16),
            pltpu.VMEM((4, BS, RHS), BF16),
            pltpu.VMEM((4, 2, 8, RHS), F32),
            dma((2,)), dma((2,)), dma((2,)), dma((8,)), dma((4,)), dma((4,)), dma((4,)),
            dma((32,)), dma, dma((7,)), dma((7,)), dma, dma, dma,
            dma((3,)), dma((3,)), dma((8,)), dma((4,)), dma((3,)), dma((4,)),
        ],
        compiler_params=pltpu.CompilerParams(
            collective_id=0, has_side_effects=True, vmem_limit_bytes=40 << 20
        ),
    )(
        block_rows.reshape(1), counts.reshape(1), rhs.reshape(2, BS, RHS), diag_inv,
        blocks.reshape(BS, BS),
    )
    return solved.reshape(1, 1, BS, RHS), rem.reshape(2, 1, BS, RHS)


def solution(mesh):
    in_specs = (
        P(None, "row", None, None),
        P(None, "row", None),
        P(None, "col", "row", None, None, None),
        P(None, "col", "row", None),
        P(None, "col", "row"),
    )
    out_specs = (P(None, "col", None, None), P(None, "row", None, None))
    return jax.shard_map(
        on_device, mesh=mesh, in_specs=in_specs, out_specs=out_specs, check_vma=False
    )
```

```python
import functools

import jax
import jax.numpy as jnp
from jax import lax
from jax.experimental import pallas as pl
from jax.experimental.pallas import tpu as pltpu
from jax.sharding import PartitionSpec as P

MESH = pl.DeviceIdType.MESH
F32 = jnp.float32
BF16 = jnp.bfloat16
NY, NZ, NX = 8, 8, 4
BS, RHS = 1024, 128
PIECE = BS // 16


def remote(src, dst, ss, rs, row, col):
    return pltpu.make_async_remote_copy(
        src_ref=src, dst_ref=dst, send_sem=ss, recv_sem=rs,
        device_id={"row": row, "col": col}, device_id_type=MESH,
    )


def kernel(brow_ref, count_ref, rhs_hbm, diag_hbm, blk_hbm, solved_ref, rem_ref,
           rhs, blk, blk2, dq, dk, dm, own, rhs_left, piv, qc, qn, qb, con, wts,
           loc, dsend, d0rec, drec, qsend, qrec, fsend, p1send, prec, p2send, p3send, p3rec, p4send, p4rec,
           xsend, xrec, hsend, hrec, wsend, wrec, bsend, brec):
    r = lax.axis_index("row")
    c = lax.axis_index("col")
    core = r % 2
    z = (r // 2) % NZ
    y = r // (2 * NZ)
    is_root = (c < 3) & (r == c + 1)
    support = ((c == 0) & ((r == 2) | (r == 3))) | ((c == 1) & (r == 3))
    early = is_root | support
    in_quarter = (r // 32) == c

    def at(yy, zz, kk):
        return (yy * NZ + zz) * 2 + kk

    drains = []

    def later(cond, *copies):
        def go():
            for copy in copies:
                copy.wait_send()

        drains.append(go if cond is None else lambda: pl.when(cond)(go))

    def finish():
        for drain in drains:
            drain()

    barrier = pltpu.get_barrier_semaphore()

    def signal(row, col):
        pl.semaphore_signal(barrier, inc=1, device_id={"row": row, "col": col}, device_id_type=MESH)

    @pl.when(is_root)
    def _():
        def body(i, carry):
            signal((r + i) % 128, c)
            return carry

        lax.fori_loop(1, 128, body, 0)

    @pl.when(r == 0)
    def _():
        def body(i, carry):
            @pl.when((c > 0) | (i > 0))
            def _():
                signal(32 * c + i, c)
            return carry

        lax.fori_loop(0, 32, body, 0)

    @pl.when(y == 0)
    def _():
        @pl.when(c == 0)
        def _():
            for cc in range(NX):
                @pl.when((r > 0) | (cc > 0))
                def _():
                    signal(0, cc)

        @pl.when(c == 1)
        def _():
            signal(1, 0)

        @pl.when(c == 2)
        def _():
            signal(2, 1)

        @pl.when(c % 2 == 1)
        def _():
            signal(3, 2)

    for d in range(1, 8):
        signal(at((y + d) % NY, z, core), c)
        signal(at(y, (z + d) % NZ, core), c)
        signal(at(y, (z + d) % NZ, 1 - core), c)
    signal(at(y, z, 1 - core), c)
    for d in range(1, 4):
        signal(r, (c + d) % NX)

    load_rhs = pltpu.make_async_copy(rhs_hbm, rhs, loc.at[0])
    load_blk = pltpu.make_async_copy(blk_hbm, blk, loc.at[1])
    load_rhs.start()
    load_blk.start()

    k_row = brow_ref[0]
    glob = k_row * 128 + r
    valid = (count_ref[0] > 0) & (glob > c)
    for i in range(2):
        w = jnp.where(valid & (k_row == i), F32(1.0), F32(0.0))
        wts[c, i] = jnp.full((8, RHS), w, F32)

    need = 25 + jnp.where((c < 3) & jnp.logical_not(is_root), 1, 0)
    need = need + jnp.where(in_quarter & (r > 0), 1, 0)
    need = need + jnp.where(r == 0, jnp.where(c == 0, 15, 16), 0)
    need = need + jnp.where(is_root, jnp.where(c == 2, 32, 16), 0)
    pl.semaphore_wait(barrier, need)

    for yy in range(NY):
        width = pl.ds(0, 128 * (yy + 1))

        @pl.when((y == yy) & in_quarter)
        def _():
            @pl.when(r > 0)
            def _():
                remote(diag_hbm.at[0, :, width], dq.at[r % 32, :, width], dsend.at[0], d0rec.at[yy % 2], 0, c).start()

            @pl.when(r == 0)
            def _():
                pltpu.make_async_copy(diag_hbm.at[0, :, width], dq.at[r % 32, :, width], d0rec.at[yy % 2]).start()

        @pl.when((y == yy) & (c < 3))
        def _():
            @pl.when(jnp.logical_not(is_root))
            def _():
                remote(diag_hbm.at[c + 1, :, width], dk.at[r, :, width], dsend.at[1], drec.at[yy], c + 1, c).start()

            @pl.when(is_root)
            def _():
                pltpu.make_async_copy(diag_hbm.at[c + 1, :, width], dk.at[r, :, width], drec.at[yy]).start()

        later((y == yy) & in_quarter & (r > 0),
              remote(diag_hbm.at[0, :, width], dq.at[0, :, width], dsend.at[0], d0rec.at[0], 0, c))
        later((y == yy) & (c < 3) & jnp.logical_not(is_root),
              remote(diag_hbm.at[0, :, width], dk.at[0, :, width], dsend.at[1], drec.at[0], 0, c))

    pair = (c == 3) & (r >= 4)

    @pl.when(pair)
    def _():
        remote(blk_hbm, blk2, bsend, brec, r, 1).start()

    later(pair, remote(blk_hbm, blk2, bsend, brec, r, 0))

    for d in range(1, 4):
        remote(wts.at[c], wts.at[c], wsend.at[d - 1], wrec.at[c], r, (c + d) % NX).start()

    load_rhs.wait()
    load_blk.wait()

    for d in range(3):
        later(None, remote(wts.at[0], wts.at[0], wsend.at[d], wrec.at[0], 0, c))

    def send_con(d):
        remote(con.at[c], con.at[c], xsend.at[d - 1], xrec.at[c], r, (c + d) % NX).start()

    def wait_con(j):
        pltpu.make_async_copy(con.at[j], con.at[j], xrec.at[j]).wait()

    def line(p):
        return (p % NZ) * 2 + p // NZ

    def squeeze(ref, block, width):
        part = ref[pl.ds(16 * block, 16), :, pl.ds(0, width)]
        return part.astype(F32).reshape(128, width).astype(BF16)

    def put_q(block, v):
        qn[pl.ds(2 * block, 2)] = v.astype(BF16).reshape(2, PIECE, RHS)

    for cc in range(NX):
        @pl.when((r == 0) & (c == cc))
        def _():
            piv[...] = rhs[0].astype(BF16)
            for h in range(2):
                block = 2 * cc + h
                width = 128 * (block + 1)
                sixteen = dq.at[pl.ds(16 * h, 16), :, pl.ds(0, width)]
                pltpu.make_async_copy(sixteen, sixteen, d0rec.at[h]).wait()
                put_q(block, jnp.dot(squeeze(dq, h, width), piv[pl.ds(0, width), :], preferred_element_type=F32))
            part = pl.ds(4 * cc, 4)
            for t in range(1, 4):
                remote(qn.at[part], qc.at[part], qsend.at[t - 1], qrec.at[cc], t, 0).start()
            for p in range(4 * cc, 4 * cc + 4):
                if p == 0:
                    pltpu.make_async_copy(qn.at[p], qb.at[0, p], prec.at[0]).start()
                else:
                    remote(qn.at[p], qb.at[0, p], p1send.at[0, p % 4], prec.at[0], line(p), 0).start()

    for p in range(4):
        later((r == 0) & ((c > 0) | (p > 0)), remote(qn.at[p], qb.at[0, p], p1send.at[0, p], prec.at[0], 0, 0))
    part0 = pl.ds(0, 4)
    later(r == 0, *[remote(qn.at[part0], qc.at[part0], qsend.at[t], qrec.at[0], 1, 0) for t in range(3)])

    @pl.when(is_root)
    def _():
        for block in range(8):
            width = 128 * (block + 1)
            sixteen = dk.at[pl.ds(16 * block, 16), :, pl.ds(0, width)]
            pltpu.make_async_copy(sixteen, sixteen, drec.at[block]).wait()
            dm[pl.ds(128 * block, 128), pl.ds(0, width)] = squeeze(dk, block, width)

    @pl.when(early)
    def _():
        for g in range(4):
            part = pl.ds(4 * g, 4)
            pltpu.make_async_copy(qc.at[part], qc.at[part], qrec.at[g]).wait()

            @pl.when((c == 1) & (r == 2))
            def _():
                remote(qc.at[part], qc.at[part], fsend.at[g], qrec.at[g], 3, 1).start()

            b = qc[part].reshape(256, RHS)

            def body(i, carry):
                at_rows = pl.ds(pl.multiple_of(i * 256, 256), 256)
                step = jnp.dot(blk[at_rows, pl.ds(256 * g, 256)], b, preferred_element_type=F32)
                own[at_rows, :] = step if g == 0 else own[at_rows, :] + step
                return carry

            lax.fori_loop(0, 4, body, 0)

    def scatter(p):
        k = c + 1
        slot = k // 2
        remote(qn.at[p], qb.at[slot, p], p1send.at[0, p], prec.at[slot], line(p), k).start()

        @pl.when(c == 2)
        def _():
            remote(qn.at[p], qb.at[slot, p], p1send.at[1, p], prec.at[slot], line(p), 1).start()

    @pl.when(is_root)
    def _():
        def body(j, carry):
            wait_con(j)
            rhs_left[...] = rhs_left[...] - con[j].astype(F32)
            return carry

        rhs_left[...] = rhs[0]
        lax.fori_loop(0, c, body, 0)
        piv[...] = (rhs_left[...] - own[...]).astype(BF16)
        for block in range(8):
            width = 128 * (block + 1)
            put_q(block, jnp.dot(dm[pl.ds(128 * block, 128), pl.ds(0, width)], piv[pl.ds(0, width), :],
                                 preferred_element_type=F32))

            @pl.when(c == 2)
            def _():
                for p in (2 * block, 2 * block + 1):
                    scatter(p)

            if block % 2 == 1:
                @pl.when(c < 2)
                def _():
                    part = pl.ds(2 * block - 2, 4)
                    remote(qn.at[part], qc.at[part], qsend.at[block // 2], qrec.at[block // 2], c + 2, c + 1).start()

    later((c == 1) & (r == 2), *[remote(qc.at[part0], qc.at[part0], fsend.at[g], qrec.at[0], 0, 0) for g in range(4)])
    later(is_root & (c < 2), *[remote(qn.at[part0], qc.at[part0], qsend.at[g], qrec.at[0], 0, 0) for g in range(4)])
    for p in range(16):
        later(is_root, remote(qn.at[p], qb.at[0, p], p1send.at[0, p], prec.at[0], 0, 3))
        later(is_root & (c == 2), remote(qn.at[p], qb.at[0, p], p1send.at[1, p], prec.at[0], 0, 3))

    @pl.when(early)
    def _():
        con[c] = own[...].astype(BF16)

    for d in (1, 2):
        @pl.when(support & (c + d == r - 1))
        def _():
            send_con(d)

    @pl.when(is_root & (c < 2))
    def _():
        for p in range(16):
            scatter(p)

    mine = core * 8 + z
    first = c < 2

    def gather(slot, active):
        @pl.when(active)
        def _():
            piece = qb.at[slot, mine]
            pltpu.make_async_copy(piece, piece, prec.at[slot]).wait()

            @pl.when(y == 0)
            def _():
                for d in (4, 3, 5, 2, 6, 1, 7):
                    remote(piece, piece, p2send.at[slot, d - 1], prec.at[slot], at(d, z, core), c).start()

            for d in (4, 3, 5, 2, 6, 1, 7):
                remote(piece, piece, p3send.at[slot, d - 1], p3rec.at[slot], at(y, (z + d) % NZ, core), c).start()
            seven = qb.at[slot, pl.ds(0, 7)]
            pltpu.make_async_copy(seven, seven, p3rec.at[slot]).wait()
            half = qb.at[slot, pl.ds(8 * core, 8)]
            remote(half, half, p4send.at[slot], p4rec.at[slot], at(y, z, 1 - core), c).start()
            other = qb.at[slot, pl.ds(8 * (1 - core), 8)]
            pltpu.make_async_copy(other, other, p4rec.at[slot]).wait()

        piece0 = qb.at[0, 0]
        half0 = qb.at[0, pl.ds(0, 8)]
        later(active & (y == 0), *[remote(piece0, piece0, p2send.at[slot, d], prec.at[slot], 0, c) for d in range(7)])
        later(active, *[remote(piece0, piece0, p3send.at[slot, d], p3rec.at[slot], 0, c) for d in range(7)])
        later(active, remote(half0, half0, p4send.at[slot], p4rec.at[slot], 0, c))

    def compute(k, a_ref, slot, t):
        at_rows = pl.ds(256 * t, 256)
        b = qb[slot].reshape(BS, RHS)
        con[k, at_rows, :] = jnp.dot(a_ref[at_rows, :], b, preferred_element_type=F32).astype(BF16)

    gather(0, first)

    @pl.when(first & jnp.logical_not(early))
    def _():
        for t in range(4):
            compute(c, blk, 0, t)

    for d in (1, 3, 2):
        @pl.when(first & jnp.logical_not(support & (c + d == r - 1)))
        def _():
            send_con(d)

    later(c < 3, *[remote(con.at[0], con.at[0], xsend.at[d], xrec.at[0], 0, c) for d in range(3)])

    @pl.when(first)
    def _():
        solved_ref[...] = qb[0].astype(F32).reshape(BS, RHS)

    gather(1, c > 0)

    def half_of(h):
        return con.at[3, pl.ds(512 * h, 512)]

    @pl.when((c == 2) & jnp.logical_not(is_root))
    def _():
        for t in range(4):
            compute(2, blk, 1, t)

    @pl.when(c == 2)
    def _():
        for d in (2, 1, 3):
            send_con(d)

    @pl.when((c == 1) & (r >= 4))
    def _():
        pltpu.make_async_copy(blk2, blk2, brec).wait()

    @pl.when((c == 1) & (r < 4))
    def _():
        con[3] = jnp.zeros((BS, RHS), BF16)

    for h in range(2):
        def tiles(which):
            for t in (2 * which, 2 * which + 1):
                if h == 0:
                    @pl.when(r >= 4)
                    def _():
                        compute(3, blk2, 1, t)
                else:
                    compute(3, blk, 1, t)

        @pl.when(c == 1 + 2 * h)
        def _():
            tiles(h)
            for d in (1, 3):
                remote(half_of(h), half_of(h), hsend.at[d // 2], hrec.at[h], r, (c + d) % NX).start()
            tiles(1 - h)

    later(c % 2 == 1, *[remote(half_of(0), half_of(0), hsend.at[d], hrec.at[0], r, 0) for d in range(2)])

    @pl.when(c >= 2)
    def _():
        solved_ref[...] = qb[1].astype(F32).reshape(BS, RHS)

    for j in range(4):
        @pl.when(c != j)
        def _():
            pltpu.make_async_copy(wts.at[j], wts.at[j], wrec.at[j]).wait()

    def update(j, base, rows):
        got = con[j, rows, :].astype(F32).reshape(rows.size // 8, 8, RHS)
        for i in range(2):
            step = (got * wts[j, i][None]).reshape(rows.size, RHS)
            rem_ref[i, rows, :] = base[i, rows, :] - step

    for j in range(3):
        @pl.when((c != j) & jnp.logical_not(is_root & (c > j)))
        def _():
            wait_con(j)

        update(j, rhs if j == 0 else rem_ref, pl.ds(0, BS))

    for h in range(2):
        @pl.when(c % 2 == 0)
        def _():
            pltpu.make_async_copy(half_of(h), half_of(h), hrec.at[h]).wait()

        update(3, rem_ref, pl.ds(512 * h, 512))

    finish()


def on_device(rhs, diag_inv, blocks, block_rows, counts):
    vmem = pl.BlockSpec(memory_space=pltpu.VMEM)
    smem = pl.BlockSpec(memory_space=pltpu.SMEM)
    hbm = pl.BlockSpec(memory_space=pltpu.HBM)
    dma = pltpu.SemaphoreType.DMA
    solved, rem = pl.pallas_call(
        kernel,
        out_shape=(
            jax.ShapeDtypeStruct((BS, RHS), F32),
            jax.ShapeDtypeStruct((2, BS, RHS), F32),
        ),
        in_specs=[smem, smem, hbm, hbm, hbm],
        out_specs=(vmem, vmem),
        scratch_shapes=[
            pltpu.VMEM((2, BS, RHS), F32),
            pltpu.VMEM((BS, BS), BF16),
            pltpu.VMEM((BS, BS), BF16),
            pltpu.VMEM((32, 8, BS), BF16),
            pltpu.VMEM((128, 8, BS), BF16),
            pltpu.VMEM((BS, BS), BF16),
            pltpu.VMEM((BS, RHS), F32),
            pltpu.VMEM((BS, RHS), F32),
            pltpu.VMEM((BS, RHS), BF16),
            pltpu.VMEM((16, PIECE, RHS), BF16),
            pltpu.VMEM((16, PIECE, RHS), BF16),
            pltpu.VMEM((2, 16, PIECE, RHS), BF16),
            pltpu.VMEM((4, BS, RHS), BF16),
            pltpu.VMEM((4, 2, 8, RHS), F32),
            dma((2,)), dma((2,)), dma((2,)), dma((8,)), dma((4,)), dma((4,)), dma((4,)),
            dma((2, 16)), dma((2,)), dma((2, 7)), dma((2, 7)), dma((2,)), dma((2,)), dma((2,)),
            dma((3,)), dma((4,)), dma((2,)), dma((2,)), dma((3,)), dma((4,)), dma, dma,
        ],
        compiler_params=pltpu.CompilerParams(
            collective_id=0, has_side_effects=True, vmem_limit_bytes=40 << 20
        ),
    )(
        block_rows.reshape(1), counts.reshape(1), rhs.reshape(2, BS, RHS), diag_inv,
        blocks.reshape(BS, BS),
    )
    return solved.reshape(1, 1, BS, RHS), rem.reshape(2, 1, BS, RHS)


def solution(mesh):
    in_specs = (
        P(None, "row", None, None),
        P(None, "row", None),
        P(None, "col", "row", None, None, None),
        P(None, "col", "row", None),
        P(None, "col", "row"),
    )
    out_specs = (P(None, "col", None, None), P(None, "row", None, None))
    return jax.shard_map(
        on_device, mesh=mesh, in_specs=in_specs, out_specs=out_specs, check_vma=False
    )
```

```python
import functools

import jax
import jax.numpy as jnp
from jax import lax
from jax.experimental import pallas as pl
from jax.experimental.pallas import tpu as pltpu
from jax.sharding import PartitionSpec as P

MESH = pl.DeviceIdType.MESH
F32 = jnp.float32
BF16 = jnp.bfloat16
NY, NZ, NX = 8, 8, 4
BS, RHS = 1024, 128
ORDER = (1, 3, 0, 2)
PIECE = BS // 16


def remote(src, dst, ss, rs, row, col):
    return pltpu.make_async_remote_copy(
        src_ref=src, dst_ref=dst, send_sem=ss, recv_sem=rs,
        device_id={"row": row, "col": col}, device_id_type=MESH,
    )


def kernel(brow_ref, count_ref, rhs_hbm, diag_hbm, blk_hbm, solved_hbm, rem_hbm,
           solved_ref, rem_ref, rhs, blk, blk2, dq, dk, dm, own, left, piv, qc, qc2, qn, qb, con, wts,
           loc, dsend, d0rec, drec, qsend, qrec, q2rec, fsend, p1send, prec, p2send, p3send, p3rec, p4send, p4rec,
           xsend, xrec, hsend, hrec, wsend, wrec, bsend, brec, turn):
    r = lax.axis_index("row")
    c = lax.axis_index("col")
    core = r % 2
    z = (r // 2) % NZ
    y = r // (2 * NZ)
    is_a = (c == 0) & (r == 1)
    is_b = (c == 1) & (r == 2)
    is_c = (c == 1) & (r == 3)
    is_root = is_a | is_b | is_c
    support = (c == 0) & ((r == 2) | (r == 3))
    early = is_root | support
    in_quarter = (r // 32) == c

    def at(yy, zz, kk):
        return (yy * NZ + zz) * 2 + kk

    drains = []

    def later(cond, *copies):
        def go():
            for copy in copies:
                copy.wait_send()

        drains.append(go if cond is None else lambda: pl.when(cond)(go))

    def finish():
        for drain in drains:
            drain()

    barrier = pltpu.get_barrier_semaphore()

    def signal(row, col):
        pl.semaphore_signal(barrier, inc=1, device_id={"row": row, "col": col}, device_id_type=MESH)

    @pl.when(is_root)
    def _():
        def body(i, carry):
            signal((r + i) % 128, c)
            return carry

        lax.fori_loop(1, 128, body, 0)

    @pl.when(r == 0)
    def _():
        def body(i, carry):
            @pl.when((c > 0) | (i > 0))
            def _():
                signal(32 * c + i, c)
            return carry

        lax.fori_loop(0, 32, body, 0)

    @pl.when(y == 0)
    def _():
        @pl.when(c == 0)
        def _():
            for cc in range(NX):
                @pl.when((r > 0) | (cc > 0))
                def _():
                    signal(0, cc)

        @pl.when(c == 1)
        def _():
            signal(1, 0)

        @pl.when(c == 2)
        def _():
            signal(2, 1)

        @pl.when((c % 2 == 1) & jnp.logical_not(is_c))
        def _():
            signal(3, 1)

    for d in range(1, 8):
        signal(at((y + d) % NY, z, core), c)
        signal(at(y, (z + d) % NZ, core), c)
        signal(at(y, (z + d) % NZ, 1 - core), c)
    signal(at(y, z, 1 - core), c)
    for d in range(1, 4):
        signal(r, (c + d) % NX)

    save_solved = pltpu.make_async_copy(solved_ref, solved_hbm, loc.at[2])
    load_rhs = pltpu.make_async_copy(rhs_hbm, rhs, loc.at[0])
    load_blk = pltpu.make_async_copy(blk_hbm, blk, loc.at[1])
    load_rhs.start()
    load_blk.start()

    k_row = jnp.broadcast_to(brow_ref[0, 0], (8, RHS))
    count = jnp.broadcast_to(count_ref[0], (8, RHS))
    valid = (count > 0) & (k_row * 128 + r > c)
    for i in range(2):
        wts[c, i] = jnp.where(valid & (k_row == i), F32(1.0), F32(0.0))

    need = 25 + jnp.where(c == 1, 2, jnp.where(c == 0, 1, 0)) - jnp.where(is_root, 1, 0)
    need = need + jnp.where(in_quarter & (r > 0), 1, 0)
    need = need + jnp.where(r == 0, jnp.where(c == 0, 15, 16), 0)
    need = need + jnp.where(is_c, 31, jnp.where(is_root, 16, 0))
    pl.semaphore_wait(barrier, need)

    for yy in range(NY):
        width = pl.ds(0, 128 * (yy + 1))

        @pl.when((y == yy) & in_quarter)
        def _():
            @pl.when(r > 0)
            def _():
                remote(diag_hbm.at[0, :, width], dq.at[r % 32, :, width], dsend.at[0], d0rec.at[yy % 2], 0, c).start()

            @pl.when(r == 0)
            def _():
                pltpu.make_async_copy(diag_hbm.at[0, :, width], dq.at[r % 32, :, width], d0rec.at[yy % 2]).start()

        later((y == yy) & in_quarter & (r > 0),
              remote(diag_hbm.at[0, :, width], dq.at[0, :, width], dsend.at[0], d0rec.at[0], 0, c))

    def send_diag(plane, k, slot):
        for yy in range(NY):
            width = pl.ds(0, 128 * (yy + 1))
            src = diag_hbm.at[k, :, width]

            @pl.when((y == yy) & (c == plane) & (r != k))
            def _():
                remote(src, dk.at[r, :, width], dsend.at[slot], drec.at[yy], k, plane).start()

            if yy == 0:
                @pl.when((c == plane) & (r == k))
                def _():
                    pltpu.make_async_copy(src, dk.at[r, :, width], drec.at[yy]).start()

            later((y == yy) & (c == plane) & (r != k),
                  remote(src, dk.at[0, :, width], dsend.at[slot], drec.at[0], 0, c))

    send_diag(0, 1, 1)

    for d in range(1, 4):
        remote(wts.at[c], wts.at[c], wsend.at[d - 1], wrec.at[c], r, (c + d) % NX).start()

    pair = (c == 3) & (r >= 4)
    lend = (c == 2) & (r == 3)

    @pl.when(pair | lend)
    def _():
        remote(blk_hbm, blk2, bsend, brec, r, 1).start()

    later(pair | lend, remote(blk_hbm, blk2, bsend, brec, r, 0))

    for j in range(4):
        @pl.when(c != j)
        def _():
            pltpu.make_async_copy(wts.at[j], wts.at[j], wrec.at[j]).wait()

    send_diag(1, 2, 1)
    send_diag(1, 3, 2)
    load_rhs.wait()
    load_blk.wait()

    for d in range(3):
        later(None, remote(wts.at[0], wts.at[0], wsend.at[d], wrec.at[0], 0, c))

    def send_con(d):
        remote(con.at[c], con.at[c], xsend.at[d - 1], xrec.at[c], r, (c + d) % NX).start()

    def wait_con(j):
        pltpu.make_async_copy(con.at[j], con.at[j], xrec.at[j]).wait()

    def line(p):
        return (p % NZ) * 2 + p // NZ

    def squeeze(ref, block, width):
        part = ref[pl.ds(16 * block, 16), :, pl.ds(0, width)]
        return part.astype(F32).reshape(128, width).astype(BF16)

    def put_q(block, v):
        qn[pl.ds(2 * block, 2)] = v.astype(BF16).reshape(2, PIECE, RHS)

    for cc in range(NX):
        @pl.when((r == 0) & (c == cc))
        def _():
            piv[...] = rhs[0].astype(BF16)
            for h in range(2):
                block = 2 * cc + h
                width = 128 * (block + 1)
                sixteen = dq.at[pl.ds(16 * h, 16), :, pl.ds(0, width)]
                pltpu.make_async_copy(sixteen, sixteen, d0rec.at[h]).wait()
                put_q(block, jnp.dot(squeeze(dq, h, width), piv[pl.ds(0, width), :], preferred_element_type=F32))
            part = pl.ds(4 * cc, 4)
            for t in range(1, 4):
                remote(qn.at[part], qc.at[part], qsend.at[t - 1], qrec.at[cc], t, 0).start()
            for p in range(4 * cc, 4 * cc + 4):
                if p == 0:
                    pltpu.make_async_copy(qn.at[p], qb.at[0, p], prec.at[0]).start()
                else:
                    remote(qn.at[p], qb.at[0, p], p1send.at[0, p % 4], prec.at[0], line(p), 0).start()

    for p in range(4):
        later((r == 0) & ((c > 0) | (p > 0)), remote(qn.at[p], qb.at[0, p], p1send.at[0, p], prec.at[0], 0, 0))
    part0 = pl.ds(0, 4)
    later(r == 0, *[remote(qn.at[part0], qc.at[part0], qsend.at[t], qrec.at[0], 1, 0) for t in range(3)])

    @pl.when(is_root)
    def _():
        for block in range(8):
            width = 128 * (block + 1)
            sixteen = dk.at[pl.ds(16 * block, 16), :, pl.ds(0, width)]
            pltpu.make_async_copy(sixteen, sixteen, drec.at[block]).wait()
            dm[pl.ds(128 * block, 128), pl.ds(0, width)] = squeeze(dk, block, width)

    def times(a_ref, q_ref, g, put):
        b = q_ref[pl.ds(4 * g, 4)].reshape(256, RHS)

        def body(i, carry):
            at_rows = pl.ds(pl.multiple_of(i * 256, 256), 256)
            put(at_rows, jnp.dot(a_ref[at_rows, pl.ds(256 * g, 256)], b, preferred_element_type=F32))
            return carry

        lax.fori_loop(0, 4, body, 0)

    @pl.when(early)
    def _():
        for n, g in enumerate(ORDER):
            part = pl.ds(4 * g, 4)
            pltpu.make_async_copy(qc.at[part], qc.at[part], qrec.at[g]).wait()

            @pl.when(is_b)
            def _():
                remote(qc.at[part], qc.at[part], fsend.at[g], qrec.at[g], 3, 1).start()

            def put(at_rows, step):
                own[at_rows, :] = step if n == 0 else own[at_rows, :] + step

            times(blk, qc, g, put)

    @pl.when(is_a)
    def _():
        left[...] = rhs[0] - own[...]

    @pl.when(is_b | is_c)
    def _():
        wait_con(0)
        left[...] = rhs[0] - own[...] - con[0].astype(F32)

    @pl.when(is_c)
    def _():
        pltpu.make_async_copy(blk2, blk2, brec).wait()
        for g in ORDER:
            part = pl.ds(4 * g, 4)
            pltpu.make_async_copy(qc2.at[part], qc2.at[part], q2rec.at[g]).wait()

            def put(at_rows, step):
                left[at_rows, :] = left[at_rows, :] - step

            times(blk2, qc2, g, put)

    def scatter(p):
        slot = r // 2
        remote(qn.at[p], qb.at[slot, p], p1send.at[0, p], prec.at[slot], line(p), r).start()

        @pl.when(is_c)
        def _():
            if line(p) == 3:
                pltpu.make_async_copy(qn.at[p], qb.at[1, p], prec.at[1]).start()
            else:
                remote(qn.at[p], qb.at[1, p], p1send.at[1, p], prec.at[1], line(p), 1).start()

    @pl.when(is_root)
    def _():
        piv[...] = left[...].astype(BF16)
        for g in ORDER:
            for block in (2 * g, 2 * g + 1):
                width = 128 * (block + 1)
                put_q(block, jnp.dot(dm[pl.ds(128 * block, 128), pl.ds(0, width)], piv[pl.ds(0, width), :],
                                     preferred_element_type=F32))

                @pl.when(is_c)
                def _():
                    scatter(2 * block)
                    scatter(2 * block + 1)

            part = pl.ds(4 * g, 4)

            @pl.when(is_a)
            def _():
                remote(qn.at[part], qc.at[part], qsend.at[g], qrec.at[g], 2, 1).start()

            @pl.when(is_b)
            def _():
                remote(qn.at[part], qc2.at[part], qsend.at[g], q2rec.at[g], 3, 1).start()
                for p in range(4 * g, 4 * g + 4):
                    scatter(p)

    later(is_b, *[remote(qc.at[part0], qc.at[part0], fsend.at[g], qrec.at[0], 0, 0) for g in range(4)])
    later(is_a | is_b, *[remote(qn.at[part0], qc.at[part0], qsend.at[g], qrec.at[0], 0, 0) for g in range(4)])
    for p in range(16):
        later(is_root, remote(qn.at[p], qb.at[0, p], p1send.at[0, p], prec.at[0], 0, 3))
        if line(p) != 3:
            later(is_c, remote(qn.at[p], qb.at[0, p], p1send.at[1, p], prec.at[0], 0, 3))

    @pl.when(early)
    def _():
        con[c] = own[...].astype(BF16)

    @pl.when(support)
    def _():
        @pl.when(r == 3)
        def _():
            pl.semaphore_wait(turn, 1)

        send_con(1)

        @pl.when(r == 2)
        def _():
            remote(con.at[0], con.at[0], xsend.at[0], xrec.at[0], 0, c).wait_send()
            pl.semaphore_signal(turn, inc=1, device_id={"row": 3, "col": 0}, device_id_type=MESH)

    @pl.when(is_a)
    def _():
        for p in range(16):
            scatter(p)

    mine = core * 8 + z
    first = c < 2

    def gather(slot, active):
        @pl.when(active)
        def _():
            piece = qb.at[slot, mine]
            pltpu.make_async_copy(piece, piece, prec.at[slot]).wait()

            @pl.when(y == 0)
            def _():
                for d in (4, 3, 5, 2, 6, 1, 7):
                    remote(piece, piece, p2send.at[slot, d - 1], prec.at[slot], at(d, z, core), c).start()

            for d in (4, 3, 5, 2, 6, 1, 7):
                remote(piece, piece, p3send.at[slot, d - 1], p3rec.at[slot], at(y, (z + d) % NZ, core), c).start()
            seven = qb.at[slot, pl.ds(0, 7)]
            pltpu.make_async_copy(seven, seven, p3rec.at[slot]).wait()
            half = qb.at[slot, pl.ds(8 * core, 8)]
            remote(half, half, p4send.at[slot], p4rec.at[slot], at(y, z, 1 - core), c).start()
            other = qb.at[slot, pl.ds(8 * (1 - core), 8)]
            pltpu.make_async_copy(other, other, p4rec.at[slot]).wait()

        piece0 = qb.at[0, 0]
        half0 = qb.at[0, pl.ds(0, 8)]
        later(active & (y == 0), *[remote(piece0, piece0, p2send.at[slot, d], prec.at[slot], 0, c) for d in range(7)])
        later(active, *[remote(piece0, piece0, p3send.at[slot, d], p3rec.at[slot], 0, c) for d in range(7)])
        later(active, remote(half0, half0, p4send.at[slot], p4rec.at[slot], 0, c))

    def compute(k, a_ref, slot, t):
        at_rows = pl.ds(256 * t, 256)
        b = qb[slot].reshape(BS, RHS)
        con[k, at_rows, :] = jnp.dot(a_ref[at_rows, :], b, preferred_element_type=F32).astype(BF16)

    gather(0, first)

    @pl.when(first & jnp.logical_not(early))
    def _():
        for t in range(4):
            compute(c, blk, 0, t)

    for d in (1, 3, 2):
        @pl.when(first & jnp.logical_not(support & (d == 1)))
        def _():
            send_con(d)

    later((c < 3) & ((c > 0) | (r != 2)), remote(con.at[0], con.at[0], xsend.at[0], xrec.at[0], 0, c))
    later(c < 3, *[remote(con.at[0], con.at[0], xsend.at[d], xrec.at[0], 0, c) for d in (1, 2)])

    @pl.when(first)
    def _():
        solved_ref[...] = qb[0].astype(F32).reshape(BS, RHS)
        save_solved.start()

    gather(1, c > 0)

    def tile_of(t):
        return con.at[3, pl.ds(256 * t, 256)]

    @pl.when(c == 2)
    def _():
        for t in range(4):
            compute(2, blk, 1, t)

    @pl.when(c == 2)
    def _():
        for d in (2, 1, 3):
            send_con(d)

    @pl.when((c == 1) & (r >= 4))
    def _():
        pltpu.make_async_copy(blk2, blk2, brec).wait()

    @pl.when((c == 1) & (r < 4))
    def _():
        con[3] = jnp.zeros((BS, RHS), BF16)

    for h in range(2):
        def tile(t):
            if h == 0:
                @pl.when(r >= 4)
                def _():
                    compute(3, blk2, 1, t)
            else:
                compute(3, blk, 1, t)

        @pl.when(c == 1 + 2 * h)
        def _():
            for t in (2 * h, 2 * h + 1):
                tile(t)
                for d in (1, 3):
                    remote(tile_of(t), tile_of(t), hsend.at[d // 2, t % 2], hrec.at[t], r, (c + d) % NX).start()
            for t in (2 - 2 * h, 3 - 2 * h):
                tile(t)

    later(c % 2 == 1, *[remote(tile_of(0), tile_of(0), hsend.at[d, t], hrec.at[0], r, 0) for d in range(2) for t in range(2)])

    @pl.when(c >= 2)
    def _():
        solved_ref[...] = qb[1].astype(F32).reshape(BS, RHS)
        save_solved.start()

    def update(j, base, rows):
        got = con[j, rows, :].astype(F32).reshape(rows.size // 8, 8, RHS)
        for i in range(2):
            step = (got * wts[j, i][None]).reshape(rows.size, RHS)
            rem_ref[i, rows, :] = base[i, rows, :] - step

    for j in range(3):
        @pl.when((c != j) & jnp.logical_not((is_b | is_c) & (j == 0)))
        def _():
            wait_con(j)

        update(j, rhs if j == 0 else rem_ref, pl.ds(0, BS))

    for n, t in enumerate((0, 2, 1, 3)):
        @pl.when(c % 2 == 0)
        def _():
            pltpu.make_async_copy(tile_of(t), tile_of(t), hrec.at[t]).wait()

        rows = pl.ds(256 * t, 256)
        update(3, rem_ref, rows)
        pltpu.make_async_copy(rem_ref.at[:, rows], rem_hbm.at[:, rows], loc.at[3 + t]).start()

    for t in range(4):
        rows = pl.ds(256 * t, 256)
        pltpu.make_async_copy(rem_ref.at[:, rows], rem_hbm.at[:, rows], loc.at[3 + t]).wait()
    save_solved.wait()
    finish()


def hand_over(solved_in, rem_in, solved_out, rem_out, buf, sems):
    moves = [(solved_in, solved_out)]
    moves += [(rem_in.at[i], rem_out.at[i, 0]) for i in range(2)]
    moves = [(a.at[pl.ds(512 * h, 512)], (b.at[0, 0] if n == 0 else b).at[pl.ds(512 * h, 512)])
             for n, (a, b) in enumerate(moves) for h in range(2)]
    reads = [pltpu.make_async_copy(a, buf.at[n], sems.at[0, n]) for n, (a, b) in enumerate(moves)]
    writes = [pltpu.make_async_copy(buf.at[n], b, sems.at[1, n]) for n, (a, b) in enumerate(moves)]
    for read in reads:
        read.start()
    for read, write in zip(reads, writes):
        read.wait()
        write.start()
    for write in writes:
        write.wait()


def on_device(rhs, diag_inv, blocks, block_rows, counts):
    vmem = pl.BlockSpec(memory_space=pltpu.VMEM)
    hbm = pl.BlockSpec(memory_space=pltpu.HBM)
    dma = pltpu.SemaphoreType.DMA
    solved, rem = pl.pallas_call(
        kernel,
        out_shape=(
            jax.ShapeDtypeStruct((BS, RHS), F32),
            jax.ShapeDtypeStruct((2, BS, RHS), F32),
        ),
        in_specs=[vmem, vmem, hbm, hbm, hbm],
        out_specs=(hbm, hbm),
        scratch_shapes=[
            pltpu.VMEM((BS, RHS), F32),
            pltpu.VMEM((2, BS, RHS), F32),
            pltpu.VMEM((2, BS, RHS), F32),
            pltpu.VMEM((BS, BS), BF16),
            pltpu.VMEM((BS, BS), BF16),
            pltpu.VMEM((32, 8, BS), BF16),
            pltpu.VMEM((128, 8, BS), BF16),
            pltpu.VMEM((BS, BS), BF16),
            pltpu.VMEM((BS, RHS), F32),
            pltpu.VMEM((BS, RHS), F32),
            pltpu.VMEM((BS, RHS), BF16),
            pltpu.VMEM((16, PIECE, RHS), BF16),
            pltpu.VMEM((16, PIECE, RHS), BF16),
            pltpu.VMEM((16, PIECE, RHS), BF16),
            pltpu.VMEM((2, 16, PIECE, RHS), BF16),
            pltpu.VMEM((4, BS, RHS), BF16),
            pltpu.VMEM((4, 2, 8, RHS), F32),
            dma((7,)), dma((3,)), dma((2,)), dma((8,)), dma((4,)), dma((4,)), dma((4,)), dma((4,)),
            dma((2, 16)), dma((2,)), dma((2, 7)), dma((2, 7)), dma((2,)), dma((2,)), dma((2,)),
            dma((3,)), dma((4,)), dma((2, 2)), dma((4,)), dma((3,)), dma((4,)), dma, dma, pltpu.SemaphoreType.REGULAR,
        ],
        compiler_params=pltpu.CompilerParams(
            collective_id=0, has_side_effects=True, vmem_limit_bytes=63 << 20
        ),
    )(
        block_rows, counts, rhs.reshape(2, BS, RHS), diag_inv,
        blocks.reshape(BS, BS),
    )
    return pl.pallas_call(
        hand_over,
        out_shape=(
            jax.ShapeDtypeStruct((1, 1, BS, RHS), F32),
            jax.ShapeDtypeStruct((2, 1, BS, RHS), F32),
        ),
        in_specs=[hbm, hbm],
        out_specs=(hbm, hbm),
        scratch_shapes=[pltpu.VMEM((6, BS // 2, RHS), F32), dma((2, 6))],
        compiler_params=pltpu.CompilerParams(vmem_limit_bytes=63 << 20),
    )(solved, rem)


def solution(mesh):
    in_specs = (
        P(None, "row", None, None),
        P(None, "row", None),
        P(None, "col", "row", None, None, None),
        P(None, "col", "row", None),
        P(None, "col", "row"),
    )
    out_specs = (P(None, "col", None, None), P(None, "row", None, None))
    return jax.shard_map(
        on_device, mesh=mesh, in_specs=in_specs, out_specs=out_specs, check_vma=False
    )
```

```python
import functools

import jax
import jax.numpy as jnp
from jax import lax
from jax.experimental import pallas as pl
from jax.experimental.pallas import tpu as pltpu
from jax.sharding import PartitionSpec as P

MESH = pl.DeviceIdType.MESH
F32 = jnp.float32
BF16 = jnp.bfloat16
NY, NZ, NX = 8, 8, 4
BS, RHS = 1024, 128
ORDER = (1, 3, 0, 2)
PIECE = BS // 16


def remote(src, dst, ss, rs, row, col):
    return pltpu.make_async_remote_copy(
        src_ref=src, dst_ref=dst, send_sem=ss, recv_sem=rs,
        device_id={"row": row, "col": col}, device_id_type=MESH,
    )


def kernel(brow_ref, count_ref, rhs_hbm, diag_hbm, blk_hbm, solved_ref, rem_ref,
           rhs, blk, blk2, dq, dk, dm, own, left, piv, qc, qc2, qn, qb, con, wts,
           loc, dsend, d0rec, drec, qsend, qrec, q2rec, fsend, p1send, prec, p2send, p3send, p3rec, p4send, p4rec,
           xsend, xrec, hsend, hrec, wsend, wrec, bsend, brec, turn):
    r = lax.axis_index("row")
    c = lax.axis_index("col")
    core = r % 2
    z = (r // 2) % NZ
    y = r // (2 * NZ)
    is_a = (c == 0) & (r == 1)
    is_b = (c == 1) & (r == 2)
    is_c = (c == 1) & (r == 3)
    is_root = is_a | is_b | is_c
    support = (c == 0) & ((r == 2) | (r == 3))
    early = is_root | support
    in_quarter = (r // 32) == c

    def at(yy, zz, kk):
        return (yy * NZ + zz) * 2 + kk

    drains = []

    def later(cond, *copies):
        def go():
            for copy in copies:
                copy.wait_send()

        drains.append(go if cond is None else lambda: pl.when(cond)(go))

    def finish():
        for drain in drains:
            drain()

    barrier = pltpu.get_barrier_semaphore()

    def signal(row, col):
        pl.semaphore_signal(barrier, inc=1, device_id={"row": row, "col": col}, device_id_type=MESH)

    @pl.when(is_root)
    def _():
        def body(i, carry):
            signal((r + i) % 128, c)
            return carry

        lax.fori_loop(1, 128, body, 0)

    @pl.when(r == 0)
    def _():
        def body(i, carry):
            @pl.when((c > 0) | (i > 0))
            def _():
                signal(32 * c + i, c)
            return carry

        lax.fori_loop(0, 32, body, 0)

    @pl.when(y == 0)
    def _():
        @pl.when(c == 0)
        def _():
            for cc in range(NX):
                @pl.when((r > 0) | (cc > 0))
                def _():
                    signal(0, cc)

        @pl.when(c == 1)
        def _():
            signal(1, 0)

        @pl.when(c == 2)
        def _():
            signal(2, 1)

        @pl.when((c % 2 == 1) & jnp.logical_not(is_c))
        def _():
            signal(3, 1)

    for d in range(1, 8):
        signal(at((y + d) % NY, z, core), c)
        signal(at(y, (z + d) % NZ, core), c)
        signal(at(y, (z + d) % NZ, 1 - core), c)
    signal(at(y, z, 1 - core), c)
    for d in range(1, 4):
        signal(r, (c + d) % NX)

    load_rhs = pltpu.make_async_copy(rhs_hbm, rhs, loc.at[0])
    load_blk = pltpu.make_async_copy(blk_hbm, blk, loc.at[1])
    load_rhs.start()
    load_blk.start()

    k_row = jnp.broadcast_to(brow_ref[0, 0], (8, RHS))
    count = jnp.broadcast_to(count_ref[0], (8, RHS))
    valid = (count > 0) & (k_row * 128 + r > c)
    for i in range(2):
        wts[c, i] = jnp.where(valid & (k_row == i), F32(1.0), F32(0.0))

    need = 25 + jnp.where(c == 1, 2, jnp.where(c == 0, 1, 0)) - jnp.where(is_root, 1, 0)
    need = need + jnp.where(in_quarter & (r > 0), 1, 0)
    need = need + jnp.where(r == 0, jnp.where(c == 0, 15, 16), 0)
    need = need + jnp.where(is_c, 31, jnp.where(is_root, 16, 0))
    pl.semaphore_wait(barrier, need)

    for yy in range(NY):
        width = pl.ds(0, 128 * (yy + 1))

        @pl.when((y == yy) & in_quarter)
        def _():
            @pl.when(r > 0)
            def _():
                remote(diag_hbm.at[0, :, width], dq.at[r % 32, :, width], dsend.at[0], d0rec.at[yy % 2], 0, c).start()

            @pl.when(r == 0)
            def _():
                pltpu.make_async_copy(diag_hbm.at[0, :, width], dq.at[r % 32, :, width], d0rec.at[yy % 2]).start()

        later((y == yy) & in_quarter & (r > 0),
              remote(diag_hbm.at[0, :, width], dq.at[0, :, width], dsend.at[0], d0rec.at[0], 0, c))

    def send_diag(plane, k, slot):
        for yy in range(NY):
            width = pl.ds(0, 128 * (yy + 1))
            src = diag_hbm.at[k, :, width]

            @pl.when((y == yy) & (c == plane) & (r != k))
            def _():
                remote(src, dk.at[r, :, width], dsend.at[slot], drec.at[yy], k, plane).start()

            if yy == 0:
                @pl.when((c == plane) & (r == k))
                def _():
                    pltpu.make_async_copy(src, dk.at[r, :, width], drec.at[yy]).start()

            later((y == yy) & (c == plane) & (r != k),
                  remote(src, dk.at[0, :, width], dsend.at[slot], drec.at[0], 0, c))

    send_diag(0, 1, 1)

    for d in range(1, 4):
        remote(wts.at[c], wts.at[c], wsend.at[d - 1], wrec.at[c], r, (c + d) % NX).start()

    pair = (c == 3) & (r >= 4)
    lend = (c == 2) & (r == 3)

    @pl.when(pair | lend)
    def _():
        remote(blk_hbm, blk2, bsend, brec, r, 1).start()

    later(pair | lend, remote(blk_hbm, blk2, bsend, brec, r, 0))

    for j in range(4):
        @pl.when(c != j)
        def _():
            pltpu.make_async_copy(wts.at[j], wts.at[j], wrec.at[j]).wait()

    send_diag(1, 2, 1)
    send_diag(1, 3, 2)
    load_rhs.wait()
    load_blk.wait()

    for d in range(3):
        later(None, remote(wts.at[0], wts.at[0], wsend.at[d], wrec.at[0], 0, c))

    def send_con(d):
        remote(con.at[c], con.at[c], xsend.at[d - 1], xrec.at[c], r, (c + d) % NX).start()

    def wait_con(j):
        pltpu.make_async_copy(con.at[j], con.at[j], xrec.at[j]).wait()

    def line(p):
        return (p % NZ) * 2 + p // NZ

    def squeeze(ref, block, width):
        part = ref[pl.ds(16 * block, 16), :, pl.ds(0, width)]
        return part.astype(F32).reshape(128, width).astype(BF16)

    def put_q(block, v):
        qn[pl.ds(2 * block, 2)] = v.astype(BF16).reshape(2, PIECE, RHS)

    for cc in range(NX):
        @pl.when((r == 0) & (c == cc))
        def _():
            piv[...] = rhs[0].astype(BF16)
            for h in range(2):
                block = 2 * cc + h
                width = 128 * (block + 1)
                sixteen = dq.at[pl.ds(16 * h, 16), :, pl.ds(0, width)]
                pltpu.make_async_copy(sixteen, sixteen, d0rec.at[h]).wait()
                put_q(block, jnp.dot(squeeze(dq, h, width), piv[pl.ds(0, width), :], preferred_element_type=F32))
            part = pl.ds(4 * cc, 4)
            for t in range(1, 4):
                remote(qn.at[part], qc.at[part], qsend.at[t - 1], qrec.at[cc], t, 0).start()
            for p in range(4 * cc, 4 * cc + 4):
                if p == 0:
                    pltpu.make_async_copy(qn.at[p], qb.at[0, p], prec.at[0]).start()
                else:
                    remote(qn.at[p], qb.at[0, p], p1send.at[0, p % 4], prec.at[0], line(p), 0).start()

    for p in range(4):
        later((r == 0) & ((c > 0) | (p > 0)), remote(qn.at[p], qb.at[0, p], p1send.at[0, p], prec.at[0], 0, 0))
    part0 = pl.ds(0, 4)
    later(r == 0, *[remote(qn.at[part0], qc.at[part0], qsend.at[t], qrec.at[0], 1, 0) for t in range(3)])

    @pl.when(is_root)
    def _():
        for block in range(8):
            width = 128 * (block + 1)
            sixteen = dk.at[pl.ds(16 * block, 16), :, pl.ds(0, width)]
            pltpu.make_async_copy(sixteen, sixteen, drec.at[block]).wait()
            dm[pl.ds(128 * block, 128), pl.ds(0, width)] = squeeze(dk, block, width)

    def times(a_ref, q_ref, g, put):
        b = q_ref[pl.ds(4 * g, 4)].reshape(256, RHS)

        def body(i, carry):
            at_rows = pl.ds(pl.multiple_of(i * 256, 256), 256)
            put(at_rows, jnp.dot(a_ref[at_rows, pl.ds(256 * g, 256)], b, preferred_element_type=F32))
            return carry

        lax.fori_loop(0, 4, body, 0)

    @pl.when(early)
    def _():
        for n, g in enumerate(ORDER):
            part = pl.ds(4 * g, 4)
            pltpu.make_async_copy(qc.at[part], qc.at[part], qrec.at[g]).wait()

            @pl.when(is_b)
            def _():
                remote(qc.at[part], qc.at[part], fsend.at[g], qrec.at[g], 3, 1).start()

            def put(at_rows, step):
                own[at_rows, :] = step if n == 0 else own[at_rows, :] + step

            times(blk, qc, g, put)

    @pl.when(is_a)
    def _():
        left[...] = rhs[0] - own[...]

    @pl.when(is_b | is_c)
    def _():
        wait_con(0)
        left[...] = rhs[0] - own[...] - con[0].astype(F32)

    @pl.when(is_c)
    def _():
        pltpu.make_async_copy(blk2, blk2, brec).wait()
        for g in ORDER:
            part = pl.ds(4 * g, 4)
            pltpu.make_async_copy(qc2.at[part], qc2.at[part], q2rec.at[g]).wait()

            def put(at_rows, step):
                left[at_rows, :] = left[at_rows, :] - step

            times(blk2, qc2, g, put)

    def scatter(p):
        slot = r // 2
        remote(qn.at[p], qb.at[slot, p], p1send.at[0, p], prec.at[slot], line(p), r).start()

        @pl.when(is_c)
        def _():
            if line(p) == 3:
                pltpu.make_async_copy(qn.at[p], qb.at[1, p], prec.at[1]).start()
            else:
                remote(qn.at[p], qb.at[1, p], p1send.at[1, p], prec.at[1], line(p), 1).start()

    @pl.when(is_root)
    def _():
        piv[...] = left[...].astype(BF16)
        for g in ORDER:
            for block in (2 * g, 2 * g + 1):
                width = 128 * (block + 1)
                put_q(block, jnp.dot(dm[pl.ds(128 * block, 128), pl.ds(0, width)], piv[pl.ds(0, width), :],
                                     preferred_element_type=F32))

                @pl.when(is_c)
                def _():
                    scatter(2 * block)
                    scatter(2 * block + 1)

            part = pl.ds(4 * g, 4)

            @pl.when(is_a)
            def _():
                remote(qn.at[part], qc.at[part], qsend.at[g], qrec.at[g], 2, 1).start()

            @pl.when(is_b)
            def _():
                remote(qn.at[part], qc2.at[part], qsend.at[g], q2rec.at[g], 3, 1).start()
                for p in range(4 * g, 4 * g + 4):
                    scatter(p)

    later(is_b, *[remote(qc.at[part0], qc.at[part0], fsend.at[g], qrec.at[0], 0, 0) for g in range(4)])
    later(is_a | is_b, *[remote(qn.at[part0], qc.at[part0], qsend.at[g], qrec.at[0], 0, 0) for g in range(4)])
    for p in range(16):
        later(is_root, remote(qn.at[p], qb.at[0, p], p1send.at[0, p], prec.at[0], 0, 3))
        if line(p) != 3:
            later(is_c, remote(qn.at[p], qb.at[0, p], p1send.at[1, p], prec.at[0], 0, 3))

    @pl.when(early)
    def _():
        con[c] = own[...].astype(BF16)

    @pl.when(support)
    def _():
        @pl.when(r == 3)
        def _():
            pl.semaphore_wait(turn, 1)

        send_con(1)

        @pl.when(r == 2)
        def _():
            remote(con.at[0], con.at[0], xsend.at[0], xrec.at[0], 0, c).wait_send()
            pl.semaphore_signal(turn, inc=1, device_id={"row": 3, "col": 0}, device_id_type=MESH)

    @pl.when(is_a)
    def _():
        for p in range(16):
            scatter(p)

    mine = core * 8 + z
    first = c < 2

    def gather(slot, active):
        @pl.when(active)
        def _():
            piece = qb.at[slot, mine]
            pltpu.make_async_copy(piece, piece, prec.at[slot]).wait()

            @pl.when(y == 0)
            def _():
                for d in (4, 3, 5, 2, 6, 1, 7):
                    remote(piece, piece, p2send.at[slot, d - 1], prec.at[slot], at(d, z, core), c).start()

            for d in (4, 3, 5, 2, 6, 1, 7):
                remote(piece, piece, p3send.at[slot, d - 1], p3rec.at[slot], at(y, (z + d) % NZ, core), c).start()
            seven = qb.at[slot, pl.ds(0, 7)]
            pltpu.make_async_copy(seven, seven, p3rec.at[slot]).wait()
            half = qb.at[slot, pl.ds(8 * core, 8)]
            remote(half, half, p4send.at[slot], p4rec.at[slot], at(y, z, 1 - core), c).start()
            other = qb.at[slot, pl.ds(8 * (1 - core), 8)]
            pltpu.make_async_copy(other, other, p4rec.at[slot]).wait()

        piece0 = qb.at[0, 0]
        half0 = qb.at[0, pl.ds(0, 8)]
        later(active & (y == 0), *[remote(piece0, piece0, p2send.at[slot, d], prec.at[slot], 0, c) for d in range(7)])
        later(active, *[remote(piece0, piece0, p3send.at[slot, d], p3rec.at[slot], 0, c) for d in range(7)])
        later(active, remote(half0, half0, p4send.at[slot], p4rec.at[slot], 0, c))

    def compute(k, a_ref, slot, t):
        at_rows = pl.ds(256 * t, 256)
        b = qb[slot].reshape(BS, RHS)
        con[k, at_rows, :] = jnp.dot(a_ref[at_rows, :], b, preferred_element_type=F32).astype(BF16)

    gather(0, first)

    @pl.when(first & jnp.logical_not(early))
    def _():
        for t in range(4):
            compute(c, blk, 0, t)

    for d in (1, 3, 2):
        @pl.when(first & jnp.logical_not(support & (d == 1)))
        def _():
            send_con(d)

    later((c < 3) & ((c > 0) | (r != 2)), remote(con.at[0], con.at[0], xsend.at[0], xrec.at[0], 0, c))
    later(c < 3, *[remote(con.at[0], con.at[0], xsend.at[d], xrec.at[0], 0, c) for d in (1, 2)])

    @pl.when(first)
    def _():
        solved_ref[...] = qb[0].astype(F32).reshape(BS, RHS)

    gather(1, c > 0)

    def tile_of(t):
        return con.at[3, pl.ds(256 * t, 256)]

    @pl.when(c == 2)
    def _():
        for t in range(4):
            compute(2, blk, 1, t)

    @pl.when(c == 2)
    def _():
        for d in (2, 1, 3):
            send_con(d)

    @pl.when((c == 1) & (r >= 4))
    def _():
        pltpu.make_async_copy(blk2, blk2, brec).wait()

    @pl.when((c == 1) & (r < 4))
    def _():
        con[3] = jnp.zeros((BS, RHS), BF16)

    for h in range(2):
        def tile(t):
            if h == 0:
                @pl.when(r >= 4)
                def _():
                    compute(3, blk2, 1, t)
            else:
                compute(3, blk, 1, t)

        @pl.when(c == 1 + 2 * h)
        def _():
            for t in (2 * h, 2 * h + 1):
                tile(t)
                for d in (1, 3):
                    remote(tile_of(t), tile_of(t), hsend.at[d // 2, t % 2], hrec.at[t], r, (c + d) % NX).start()
            for t in (2 - 2 * h, 3 - 2 * h):
                tile(t)

    later(c % 2 == 1, *[remote(tile_of(0), tile_of(0), hsend.at[d, t], hrec.at[0], r, 0) for d in range(2) for t in range(2)])

    @pl.when(c >= 2)
    def _():
        solved_ref[...] = qb[1].astype(F32).reshape(BS, RHS)

    def update(j, base, rows):
        got = con[j, rows, :].astype(F32).reshape(rows.size // 8, 8, RHS)
        for i in range(2):
            step = (got * wts[j, i][None]).reshape(rows.size, RHS)
            rem_ref[i, rows, :] = base[i, rows, :] - step

    for j in range(3):
        @pl.when((c != j) & jnp.logical_not((is_b | is_c) & (j == 0)))
        def _():
            wait_con(j)

        update(j, rhs if j == 0 else rem_ref, pl.ds(0, BS))

    for n, t in enumerate((0, 2, 1, 3)):
        @pl.when(c % 2 == 0)
        def _():
            pltpu.make_async_copy(tile_of(t), tile_of(t), hrec.at[t]).wait()

        update(3, rem_ref, pl.ds(256 * t, 256))

    finish()


def hand_over(solved_in, rem_in, solved_out, rem_out, sems):
    pairs = [(rem_in.at[0], rem_out.at[0, 0]), (rem_in.at[1], rem_out.at[1, 0]), (solved_in, solved_out.at[0, 0])]
    moves = []
    for n, (src, dst) in enumerate(pairs):
        for t in range(4):
            rows = pl.ds(256 * t, 256)
            moves.append(pltpu.make_async_copy(src.at[rows], dst.at[rows], sems.at[n, t]))
    for move in moves:
        move.start()
    for move in moves:
        move.wait()


def on_device(rhs, diag_inv, blocks, block_rows, counts):
    vmem = pl.BlockSpec(memory_space=pltpu.VMEM)
    hbm = pl.BlockSpec(memory_space=pltpu.HBM)
    dma = pltpu.SemaphoreType.DMA
    here = pltpu.with_memory_space_constraint
    solved, rem = pl.pallas_call(
        kernel,
        out_shape=(pltpu.VMEM((BS, RHS), F32), pltpu.VMEM((2, BS, RHS), F32)),
        in_specs=[vmem, vmem, hbm, hbm, hbm],
        out_specs=(vmem, vmem),
        scratch_shapes=[
            pltpu.VMEM((2, BS, RHS), F32),
            pltpu.VMEM((BS, BS), BF16),
            pltpu.VMEM((BS, BS), BF16),
            pltpu.VMEM((32, 8, BS), BF16),
            pltpu.VMEM((128, 8, BS), BF16),
            pltpu.VMEM((BS, BS), BF16),
            pltpu.VMEM((BS, RHS), F32),
            pltpu.VMEM((BS, RHS), F32),
            pltpu.VMEM((BS, RHS), BF16),
            pltpu.VMEM((16, PIECE, RHS), BF16),
            pltpu.VMEM((16, PIECE, RHS), BF16),
            pltpu.VMEM((16, PIECE, RHS), BF16),
            pltpu.VMEM((2, 16, PIECE, RHS), BF16),
            pltpu.VMEM((4, BS, RHS), BF16),
            pltpu.VMEM((4, 2, 8, RHS), F32),
            dma((2,)), dma((3,)), dma((2,)), dma((8,)), dma((4,)), dma((4,)), dma((4,)), dma((4,)),
            dma((2, 16)), dma((2,)), dma((2, 7)), dma((2, 7)), dma((2,)), dma((2,)), dma((2,)),
            dma((3,)), dma((4,)), dma((2, 2)), dma((4,)), dma((3,)), dma((4,)), dma, dma, pltpu.SemaphoreType.REGULAR,
        ],
        compiler_params=pltpu.CompilerParams(
            collective_id=0, has_side_effects=True, vmem_limit_bytes=40 << 20
        ),
    )(
        block_rows, counts, here(rhs.reshape(2, BS, RHS), pltpu.HBM), here(diag_inv, pltpu.HBM),
        here(blocks.reshape(BS, BS), pltpu.HBM),
    )
    return pl.pallas_call(
        hand_over,
        out_shape=(
            jax.ShapeDtypeStruct((1, 1, BS, RHS), F32),
            jax.ShapeDtypeStruct((2, 1, BS, RHS), F32),
        ),
        in_specs=[vmem, vmem],
        out_specs=(hbm, hbm),
        scratch_shapes=[dma((3, 4))],
        compiler_params=pltpu.CompilerParams(vmem_limit_bytes=4 << 20),
    )(here(solved, pltpu.VMEM), here(rem, pltpu.VMEM))


def solution(mesh):
    in_specs = (
        P(None, "row", None, None),
        P(None, "row", None),
        P(None, "col", "row", None, None, None),
        P(None, "col", "row", None),
        P(None, "col", "row"),
    )
    out_specs = (P(None, "col", None, None), P(None, "row", None, None))
    return jax.shard_map(
        on_device, mesh=mesh, in_specs=in_specs, out_specs=out_specs, check_vma=False
    )
```

```python
import functools

import jax
import jax.numpy as jnp
from jax import lax
from jax.experimental import pallas as pl
from jax.experimental.pallas import tpu as pltpu
from jax.sharding import PartitionSpec as P

MESH = pl.DeviceIdType.MESH
F32 = jnp.float32
BF16 = jnp.bfloat16
NY, NZ, NX = 8, 8, 4
BS, RHS = 1024, 128
ORDER = (1, 3, 0, 2)
PIECE = BS // 16


def remote(src, dst, ss, rs, row, col):
    return pltpu.make_async_remote_copy(
        src_ref=src, dst_ref=dst, send_sem=ss, recv_sem=rs,
        device_id={"row": row, "col": col}, device_id_type=MESH,
    )


def kernel(brow_ref, count_ref, rhs_hbm, diag_hbm, blk_hbm, solved_ref, rem_ref,
           rhs, blk, blk2, dq, dk, dm, own, left, piv, qc, qc2, qn, qb, con, wts,
           loc, dsend, d0rec, drec, qsend, qrec, q2rec, fsend, p1send, prec, p2send, p3send, p3rec, p4send, p4rec,
           xsend, xrec, h1send, h1rec, hsend, hrec, wsend, wrec, bsend, brec, turn):
    r = lax.axis_index("row")
    c = lax.axis_index("col")
    core = r % 2
    z = (r // 2) % NZ
    y = r // (2 * NZ)
    is_a = (c == 0) & (r == 1)
    is_b = (c == 1) & (r == 2)
    is_c = (c == 1) & (r == 3)
    is_root = is_a | is_b | is_c
    support = (c == 0) & ((r == 2) | (r == 3))
    early = is_root | support
    in_quarter = (r // 32) == c

    def at(yy, zz, kk):
        return (yy * NZ + zz) * 2 + kk

    drains = []

    def later(cond, *copies):
        def go():
            for copy in copies:
                copy.wait_send()

        drains.append(go if cond is None else lambda: pl.when(cond)(go))

    def finish():
        for drain in drains:
            drain()

    barrier = pltpu.get_barrier_semaphore()

    def signal(row, col):
        pl.semaphore_signal(barrier, inc=1, device_id={"row": row, "col": col}, device_id_type=MESH)

    @pl.when(is_root)
    def _():
        def body(i, carry):
            signal((r + i) % 128, c)
            return carry

        lax.fori_loop(1, 128, body, 0)

    @pl.when(r == 0)
    def _():
        def body(i, carry):
            @pl.when((c > 0) | (i > 0))
            def _():
                signal(32 * c + i, c)
            return carry

        lax.fori_loop(0, 32, body, 0)

    @pl.when(y == 0)
    def _():
        @pl.when(c == 0)
        def _():
            for cc in range(NX):
                @pl.when((r > 0) | (cc > 0))
                def _():
                    signal(0, cc)

        @pl.when(c % 2 == 1)
        def _():
            signal(1, 0)

        @pl.when(c == 2)
        def _():
            signal(2, 1)

        @pl.when((c % 2 == 1) & jnp.logical_not(is_c))
        def _():
            signal(3, 1)

    for d in range(1, 8):
        signal(at((y + d) % NY, z, core), c)
        signal(at(y, (z + d) % NZ, core), c)
        signal(at(y, (z + d) % NZ, 1 - core), c)
    signal(at(y, z, 1 - core), c)
    for d in range(1, 4):
        signal(r, (c + d) % NX)

    load_rhs = pltpu.make_async_copy(rhs_hbm, rhs, loc.at[0])
    load_blk = pltpu.make_async_copy(blk_hbm, blk, loc.at[1])
    load_rhs.start()
    load_blk.start()

    k_row = jnp.broadcast_to(brow_ref[0, 0], (8, RHS))
    count = jnp.broadcast_to(count_ref[0], (8, RHS))
    valid = (count > 0) & (k_row * 128 + r > c)
    for i in range(2):
        wts[c, i] = jnp.where(valid & (k_row == i), F32(1.0), F32(0.0))

    need = 25 + jnp.where(c == 1, 2, jnp.where(c == 0, 1, 0)) - jnp.where(is_root, 1, 0)
    need = need + jnp.where(in_quarter & (r > 0), 1, 0)
    need = need + jnp.where(r == 0, jnp.where(c == 0, 15, 16), 0)
    need = need + jnp.where(is_c, 31, jnp.where(is_a, 32, jnp.where(is_root, 16, 0)))
    pl.semaphore_wait(barrier, need)

    for yy in range(NY):
        width = pl.ds(0, 128 * (yy + 1))

        @pl.when((y == yy) & in_quarter)
        def _():
            @pl.when(r > 0)
            def _():
                remote(diag_hbm.at[0, :, width], dq.at[r % 32, :, width], dsend.at[0], d0rec.at[yy % 2], 0, c).start()

            @pl.when(r == 0)
            def _():
                pltpu.make_async_copy(diag_hbm.at[0, :, width], dq.at[r % 32, :, width], d0rec.at[yy % 2]).start()

        later((y == yy) & in_quarter & (r > 0),
              remote(diag_hbm.at[0, :, width], dq.at[0, :, width], dsend.at[0], d0rec.at[0], 0, c))

    def send_diag(plane, k, slot):
        for yy in range(NY):
            width = pl.ds(0, 128 * (yy + 1))
            src = diag_hbm.at[k, :, width]

            @pl.when((y == yy) & (c == plane) & (r != k))
            def _():
                remote(src, dk.at[r, :, width], dsend.at[slot], drec.at[yy], k, plane).start()

            if yy == 0:
                @pl.when((c == plane) & (r == k))
                def _():
                    pltpu.make_async_copy(src, dk.at[r, :, width], drec.at[yy]).start()

            later((y == yy) & (c == plane) & (r != k),
                  remote(src, dk.at[0, :, width], dsend.at[slot], drec.at[0], 0, c))

    send_diag(0, 1, 1)

    for d in range(1, 4):
        remote(wts.at[c], wts.at[c], wsend.at[d - 1], wrec.at[c], r, (c + d) % NX).start()

    pair = (c == 3) & (r >= 4)
    lend = (c == 2) & (r == 3)
    lower = pl.ds(512, 512)

    @pl.when(pair | lend)
    def _():
        remote(blk_hbm, blk2, bsend, brec, r, 1).start()

    @pl.when((c == 1) & (r >= 4))
    def _():
        remote(blk_hbm.at[lower], blk2.at[lower], bsend, brec, r, 3).start()

    later(pair | lend, remote(blk_hbm, blk2, bsend, brec, r, 0))
    later((c == 1) & (r >= 4), remote(blk_hbm.at[lower], blk2.at[lower], bsend, brec, r, 0))

    for j in range(4):
        @pl.when(c != j)
        def _():
            pltpu.make_async_copy(wts.at[j], wts.at[j], wrec.at[j]).wait()

    send_diag(1, 2, 1)
    send_diag(1, 3, 2)
    load_rhs.wait()
    load_blk.wait()

    for d in range(3):
        later(None, remote(wts.at[0], wts.at[0], wsend.at[d], wrec.at[0], 0, c))

    def send_con(d):
        remote(con.at[c], con.at[c], xsend.at[d - 1], xrec.at[c], r, (c + d) % NX).start()

    def wait_con(j):
        pltpu.make_async_copy(con.at[j], con.at[j], xrec.at[j]).wait()

    def line(p):
        return (p % NZ) * 2 + p // NZ

    def squeeze(ref, block, width):
        part = ref[pl.ds(16 * block, 16), :, pl.ds(0, width)]
        return part.astype(F32).reshape(128, width).astype(BF16)

    def put_q(block, v):
        qn[pl.ds(2 * block, 2)] = v.astype(BF16).reshape(2, PIECE, RHS)

    for cc in range(NX):
        @pl.when((r == 0) & (c == cc))
        def _():
            piv[...] = rhs[0].astype(BF16)
            for h in range(2):
                block = 2 * cc + h
                width = 128 * (block + 1)
                sixteen = dq.at[pl.ds(16 * h, 16), :, pl.ds(0, width)]
                pltpu.make_async_copy(sixteen, sixteen, d0rec.at[h]).wait()
                put_q(block, jnp.dot(squeeze(dq, h, width), piv[pl.ds(0, width), :], preferred_element_type=F32))
            part = pl.ds(4 * cc, 4)
            for t in range(1, 4):
                remote(qn.at[part], qc.at[part], qsend.at[t - 1], qrec.at[cc], t, 0).start()
            for p in range(4 * cc, 4 * cc + 4):
                if p == 0:
                    pltpu.make_async_copy(qn.at[p], qb.at[0, p], prec.at[0]).start()
                else:
                    remote(qn.at[p], qb.at[0, p], p1send.at[0, p % 4], prec.at[0], line(p), 0).start()

    for p in range(4):
        later((r == 0) & ((c > 0) | (p > 0)), remote(qn.at[p], qb.at[0, p], p1send.at[0, p], prec.at[0], 0, 0))
    part0 = pl.ds(0, 4)
    later(r == 0, *[remote(qn.at[part0], qc.at[part0], qsend.at[t], qrec.at[0], 1, 0) for t in range(3)])

    @pl.when(is_root)
    def _():
        for block in range(8):
            width = 128 * (block + 1)
            sixteen = dk.at[pl.ds(16 * block, 16), :, pl.ds(0, width)]
            pltpu.make_async_copy(sixteen, sixteen, drec.at[block]).wait()
            dm[pl.ds(128 * block, 128), pl.ds(0, width)] = squeeze(dk, block, width)

    def times(a_ref, q_ref, g, put):
        b = q_ref[pl.ds(4 * g, 4)].reshape(256, RHS)

        def body(i, carry):
            at_rows = pl.ds(pl.multiple_of(i * 256, 256), 256)
            put(at_rows, jnp.dot(a_ref[at_rows, pl.ds(256 * g, 256)], b, preferred_element_type=F32))
            return carry

        lax.fori_loop(0, 4, body, 0)

    @pl.when(early)
    def _():
        for n, g in enumerate(ORDER):
            part = pl.ds(4 * g, 4)
            pltpu.make_async_copy(qc.at[part], qc.at[part], qrec.at[g]).wait()

            @pl.when(is_b)
            def _():
                remote(qc.at[part], qc.at[part], fsend.at[g], qrec.at[g], 3, 1).start()

            def put(at_rows, step):
                own[at_rows, :] = step if n == 0 else own[at_rows, :] + step

            times(blk, qc, g, put)

    @pl.when(is_a)
    def _():
        left[...] = rhs[0] - own[...]

    @pl.when(is_b | is_c)
    def _():
        wait_con(0)
        left[...] = rhs[0] - own[...] - con[0].astype(F32)

    @pl.when(is_c)
    def _():
        pltpu.make_async_copy(blk2, blk2, brec).wait()
        for g in ORDER:
            part = pl.ds(4 * g, 4)
            pltpu.make_async_copy(qc2.at[part], qc2.at[part], q2rec.at[g]).wait()

            def put(at_rows, step):
                left[at_rows, :] = left[at_rows, :] - step

            times(blk2, qc2, g, put)

    def scatter(p):
        slot = r // 2
        remote(qn.at[p], qb.at[slot, p], p1send.at[0, p], prec.at[slot], line(p), r).start()

        @pl.when(is_a)
        def _():
            remote(qn.at[p], qb.at[0, p], p1send.at[1, p], prec.at[0], line(p), 3).start()

        @pl.when(is_c)
        def _():
            if line(p) == 3:
                pltpu.make_async_copy(qn.at[p], qb.at[1, p], prec.at[1]).start()
            else:
                remote(qn.at[p], qb.at[1, p], p1send.at[1, p], prec.at[1], line(p), 1).start()

    @pl.when(is_root)
    def _():
        piv[...] = left[...].astype(BF16)
        for g in ORDER:
            for block in (2 * g, 2 * g + 1):
                width = 128 * (block + 1)
                put_q(block, jnp.dot(dm[pl.ds(128 * block, 128), pl.ds(0, width)], piv[pl.ds(0, width), :],
                                     preferred_element_type=F32))

                @pl.when(is_c)
                def _():
                    scatter(2 * block)
                    scatter(2 * block + 1)

            part = pl.ds(4 * g, 4)

            @pl.when(is_a)
            def _():
                remote(qn.at[part], qc.at[part], qsend.at[g], qrec.at[g], 2, 1).start()

            @pl.when(is_b)
            def _():
                remote(qn.at[part], qc2.at[part], qsend.at[g], q2rec.at[g], 3, 1).start()
                for p in range(4 * g, 4 * g + 4):
                    scatter(p)

    later(is_b, *[remote(qc.at[part0], qc.at[part0], fsend.at[g], qrec.at[0], 0, 0) for g in range(4)])
    later(is_a | is_b, *[remote(qn.at[part0], qc.at[part0], qsend.at[g], qrec.at[0], 0, 0) for g in range(4)])
    for p in range(16):
        later(is_root, remote(qn.at[p], qb.at[0, p], p1send.at[0, p], prec.at[0], 0, 3))
        later(is_a, remote(qn.at[p], qb.at[0, p], p1send.at[1, p], prec.at[0], 0, 3))
        if line(p) != 3:
            later(is_c, remote(qn.at[p], qb.at[0, p], p1send.at[1, p], prec.at[0], 0, 3))

    @pl.when(early)
    def _():
        con[c] = own[...].astype(BF16)

    @pl.when(support)
    def _():
        @pl.when(r == 3)
        def _():
            pl.semaphore_wait(turn, 1)

        send_con(1)

        @pl.when(r == 2)
        def _():
            remote(con.at[0], con.at[0], xsend.at[0], xrec.at[0], 0, c).wait_send()
            pl.semaphore_signal(turn, inc=1, device_id={"row": 3, "col": 0}, device_id_type=MESH)

    @pl.when(is_a)
    def _():
        for p in range(16):
            scatter(p)

    mine = core * 8 + z
    first = c < 2

    def gather(slot, active):
        @pl.when(active)
        def _():
            piece = qb.at[slot, mine]
            pltpu.make_async_copy(piece, piece, prec.at[slot]).wait()

            @pl.when(y == 0)
            def _():
                for d in (4, 3, 5, 2, 6, 1, 7):
                    remote(piece, piece, p2send.at[slot, d - 1], prec.at[slot], at(d, z, core), c).start()

            for d in (4, 3, 5, 2, 6, 1, 7):
                remote(piece, piece, p3send.at[slot, d - 1], p3rec.at[slot], at(y, (z + d) % NZ, core), c).start()
            seven = qb.at[slot, pl.ds(0, 7)]
            pltpu.make_async_copy(seven, seven, p3rec.at[slot]).wait()
            half = qb.at[slot, pl.ds(8 * core, 8)]
            remote(half, half, p4send.at[slot], p4rec.at[slot], at(y, z, 1 - core), c).start()
            other = qb.at[slot, pl.ds(8 * (1 - core), 8)]
            pltpu.make_async_copy(other, other, p4rec.at[slot]).wait()

        piece0 = qb.at[0, 0]
        half0 = qb.at[0, pl.ds(0, 8)]
        later(active & (y == 0), *[remote(piece0, piece0, p2send.at[slot, d], prec.at[slot], 0, c) for d in range(7)])
        later(active, *[remote(piece0, piece0, p3send.at[slot, d], p3rec.at[slot], 0, c) for d in range(7)])
        later(active, remote(half0, half0, p4send.at[slot], p4rec.at[slot], 0, c))

    def compute(k, a_ref, slot, t):
        at_rows = pl.ds(256 * t, 256)
        b = qb[slot].reshape(BS, RHS)
        con[k, at_rows, :] = jnp.dot(a_ref[at_rows, :], b, preferred_element_type=F32).astype(BF16)

    def tile_of(k, t):
        return con.at[k, pl.ds(256 * t, 256)]

    def share(k, plane, a_ref, slot, which, sends, recs):
        @pl.when((c == plane) & which)
        def _():
            h = plane // 2
            for t in (2 * h, 2 * h + 1):
                compute(k, a_ref, slot, t)
                for d in (1, 3):
                    remote(tile_of(k, t), tile_of(k, t), sends.at[d // 2, t % 2], recs.at[t], r, (c + d) % NX).start()
            for t in (2 - 2 * h, 3 - 2 * h):
                compute(k, a_ref, slot, t)

    gather(0, c != 2)
    low = r < 4
    high = r >= 4

    @pl.when(first & jnp.logical_not(early) & ((c == 0) | low))
    def _():
        for t in range(4):
            compute(c, blk, 0, t)

    for d in (1, 3, 2):
        @pl.when(first & ((c == 0) | low) & jnp.logical_not(support & (d == 1)))
        def _():
            send_con(d)

    whole = (c == 0) | (c == 2) | ((c == 1) & low)
    later(whole & ((c > 0) | (r != 2)), remote(con.at[0], con.at[0], xsend.at[0], xrec.at[0], 0, c))
    later(whole, *[remote(con.at[0], con.at[0], xsend.at[d], xrec.at[0], 0, c) for d in (1, 2)])
    def give(t, d):
        remote(tile_of(1, t), tile_of(1, t), h1send.at[d - 1, t % 2], h1rec.at[t], r, (c + d) % NX).start()

    @pl.when((c == 1) & high)
    def _():
        for t in (0, 1):
            compute(1, blk, 0, t)
            for d in (2, 1, 3):
                give(t, d)
        for t in (2, 3):
            compute(1, blk, 0, t)

    @pl.when((c == 3) & high)
    def _():
        pltpu.make_async_copy(blk2.at[lower], blk2.at[lower], brec).wait()
        for t in (2, 3):
            compute(1, blk2, 0, t)
            for d in (1, 3):
                give(t, d)

    tile0 = tile_of(1, 0)
    later((c % 2 == 1) & high, *[remote(tile0, tile0, h1send.at[d, t], h1rec.at[0], r, 0) for d in (0, 2) for t in range(2)])
    later((c == 1) & high, *[remote(tile0, tile0, h1send.at[1, t], h1rec.at[0], r, 0) for t in range(2)])

    @pl.when(first)
    def _():
        solved_ref[...] = qb[0].astype(F32).reshape(BS, RHS)

    gather(1, c > 0)

    @pl.when(c == 2)
    def _():
        for t in range(4):
            compute(2, blk, 1, t)

    @pl.when(c == 2)
    def _():
        for d in (2, 1, 3):
            send_con(d)

    @pl.when((c == 1) & (r >= 4))
    def _():
        pltpu.make_async_copy(blk2, blk2, brec).wait()

    @pl.when((c == 1) & (r < 4))
    def _():
        con[3] = jnp.zeros((BS, RHS), BF16)

    share(3, 1, blk2, 1, high, hsend, hrec)

    @pl.when((c == 1) & low)
    def _():
        for t in (0, 1):
            for d in (1, 3):
                remote(tile_of(3, t), tile_of(3, t), hsend.at[d // 2, t], hrec.at[t], r, (c + d) % NX).start()

    share(3, 3, blk, 1, c == 3, hsend, hrec)
    later(c % 2 == 1, *[remote(tile_of(3, 0), tile_of(3, 0), hsend.at[d, t], hrec.at[0], r, 0) for d in range(2) for t in range(2)])

    @pl.when(c >= 2)
    def _():
        solved_ref[...] = qb[1].astype(F32).reshape(BS, RHS)

    def update(j, base, rows):
        got = con[j, rows, :].astype(F32).reshape(rows.size // 8, 8, RHS)
        for i in range(2):
            step = (got * wts[j, i][None]).reshape(rows.size, RHS)
            rem_ref[i, rows, :] = base[i, rows, :] - step

    for j in range(3):
        waits = (c != j) & jnp.logical_not((is_b | is_c) & (j == 0))

        @pl.when(waits & (low if j == 1 else c >= 0))
        def _():
            wait_con(j)

        if j == 1:
            for t in range(4):
                @pl.when((c != 1 if t < 2 else c % 2 == 0) & high)
                def _():
                    pltpu.make_async_copy(tile_of(1, t), tile_of(1, t), h1rec.at[t]).wait()

        update(j, rhs if j == 0 else rem_ref, pl.ds(0, BS))

    for n, t in enumerate((0, 2, 1, 3)):
        @pl.when(c % 2 == 0)
        def _():
            pltpu.make_async_copy(tile_of(3, t), tile_of(3, t), hrec.at[t]).wait()

        update(3, rem_ref, pl.ds(256 * t, 256))

    finish()


def hand_over(solved_in, rem_in, solved_out, rem_out, sems):
    pairs = [(rem_in.at[0], rem_out.at[0, 0]), (rem_in.at[1], rem_out.at[1, 0]), (solved_in, solved_out.at[0, 0])]
    moves = []
    for n, (src, dst) in enumerate(pairs):
        for t in range(4):
            rows = pl.ds(256 * t, 256)
            moves.append(pltpu.make_async_copy(src.at[rows], dst.at[rows], sems.at[n, t]))
    for move in moves:
        move.start()
    for move in moves:
        move.wait()


def on_device(rhs, diag_inv, blocks, block_rows, counts):
    vmem = pl.BlockSpec(memory_space=pltpu.VMEM)
    hbm = pl.BlockSpec(memory_space=pltpu.HBM)
    dma = pltpu.SemaphoreType.DMA
    here = pltpu.with_memory_space_constraint
    solved, rem = pl.pallas_call(
        kernel,
        out_shape=(pltpu.VMEM((BS, RHS), F32), pltpu.VMEM((2, BS, RHS), F32)),
        in_specs=[vmem, vmem, hbm, hbm, hbm],
        out_specs=(vmem, vmem),
        scratch_shapes=[
            pltpu.VMEM((2, BS, RHS), F32),
            pltpu.VMEM((BS, BS), BF16),
            pltpu.VMEM((BS, BS), BF16),
            pltpu.VMEM((32, 8, BS), BF16),
            pltpu.VMEM((128, 8, BS), BF16),
            pltpu.VMEM((BS, BS), BF16),
            pltpu.VMEM((BS, RHS), F32),
            pltpu.VMEM((BS, RHS), F32),
            pltpu.VMEM((BS, RHS), BF16),
            pltpu.VMEM((16, PIECE, RHS), BF16),
            pltpu.VMEM((16, PIECE, RHS), BF16),
            pltpu.VMEM((16, PIECE, RHS), BF16),
            pltpu.VMEM((2, 16, PIECE, RHS), BF16),
            pltpu.VMEM((4, BS, RHS), BF16),
            pltpu.VMEM((4, 2, 8, RHS), F32),
            dma((2,)), dma((3,)), dma((2,)), dma((8,)), dma((4,)), dma((4,)), dma((4,)), dma((4,)),
            dma((2, 16)), dma((2,)), dma((2, 7)), dma((2, 7)), dma((2,)), dma((2,)), dma((2,)),
            dma((3,)), dma((4,)), dma((3, 2)), dma((4,)), dma((2, 2)), dma((4,)), dma((3,)), dma((4,)), dma, dma, pltpu.SemaphoreType.REGULAR,
        ],
        compiler_params=pltpu.CompilerParams(
            collective_id=0, has_side_effects=True, vmem_limit_bytes=40 << 20
        ),
    )(
        block_rows, counts, here(rhs.reshape(2, BS, RHS), pltpu.HBM), here(diag_inv, pltpu.HBM),
        here(blocks.reshape(BS, BS), pltpu.HBM),
    )
    return pl.pallas_call(
        hand_over,
        out_shape=(
            jax.ShapeDtypeStruct((1, 1, BS, RHS), F32),
            jax.ShapeDtypeStruct((2, 1, BS, RHS), F32),
        ),
        in_specs=[vmem, vmem],
        out_specs=(hbm, hbm),
        scratch_shapes=[dma((3, 4))],
        compiler_params=pltpu.CompilerParams(vmem_limit_bytes=4 << 20),
    )(here(solved, pltpu.VMEM), here(rem, pltpu.VMEM))


def solution(mesh):
    in_specs = (
        P(None, "row", None, None),
        P(None, "row", None),
        P(None, "col", "row", None, None, None),
        P(None, "col", "row", None),
        P(None, "col", "row"),
    )
    out_specs = (P(None, "col", None, None), P(None, "row", None, None))
    return jax.shard_map(
        on_device, mesh=mesh, in_specs=in_specs, out_specs=out_specs, check_vma=False
    )
```

```python
import functools

import jax
import jax.numpy as jnp
from jax import lax
from jax.experimental import pallas as pl
from jax.experimental.pallas import tpu as pltpu
from jax.sharding import PartitionSpec as P

MESH = pl.DeviceIdType.MESH
F32 = jnp.float32
BF16 = jnp.bfloat16
NY, NZ, NX = 8, 8, 4
BS, RHS = 1024, 128
ORDER = (0, 2, 1, 3)
PIECE = BS // 16


def remote(src, dst, ss, rs, row, col):
    return pltpu.make_async_remote_copy(
        src_ref=src, dst_ref=dst, send_sem=ss, recv_sem=rs,
        device_id={"row": row, "col": col}, device_id_type=MESH,
    )


def kernel(brow_ref, count_ref, rhs_hbm, diag_hbm, blk_hbm, solved_ref, rem_ref,
           rhs, blk, blk2, dq, dk, dm, own, left, piv, qc, qc2, qn, qb, con, wts,
           loc, dsend, d0rec, drec, qsend, qrec, q2rec, fsend, p1send, prec, p2send, p3send, p3rec, p4send, p4rec,
           xsend, xrec, h1send, h1rec, hsend, hrec, wsend, wrec, bsend, brec, turn):
    r = lax.axis_index("row")
    c = lax.axis_index("col")
    core = r % 2
    z = (r // 2) % NZ
    y = r // (2 * NZ)
    is_a = (c == 0) & (r == 1)
    is_b = (c == 1) & (r == 2)
    is_c = (c == 1) & (r == 3)
    is_root = is_a | is_b | is_c
    support = (c == 0) & ((r == 2) | (r == 3))
    early = is_root | support
    in_quarter = (r // 32) == c

    def at(yy, zz, kk):
        return (yy * NZ + zz) * 2 + kk

    drains = []

    def later(cond, *copies):
        def go():
            for copy in copies:
                copy.wait_send()

        drains.append(go if cond is None else lambda: pl.when(cond)(go))

    def finish():
        for drain in drains:
            drain()

    barrier = pltpu.get_barrier_semaphore()

    def signal(row, col):
        pl.semaphore_signal(barrier, inc=1, device_id={"row": row, "col": col}, device_id_type=MESH)

    @pl.when(is_root)
    def _():
        def body(i, carry):
            signal((r + i) % 128, c)
            return carry

        lax.fori_loop(1, 128, body, 0)

    @pl.when(r == 0)
    def _():
        def body(i, carry):
            @pl.when((c > 0) | (i > 0))
            def _():
                signal(32 * c + i, c)
            return carry

        lax.fori_loop(0, 32, body, 0)

    @pl.when(y == 0)
    def _():
        @pl.when(c == 0)
        def _():
            for cc in range(NX):
                @pl.when((r > 0) | (cc > 0))
                def _():
                    signal(0, cc)

        @pl.when(c % 2 == 1)
        def _():
            signal(1, 0)

        @pl.when(c == 2)
        def _():
            signal(2, 1)

        @pl.when((c % 2 == 1) & jnp.logical_not(is_c))
        def _():
            signal(3, 1)

    for d in range(1, 8):
        signal(at((y + d) % NY, z, core), c)
        signal(at(y, (z + d) % NZ, core), c)
        signal(at(y, (z + d) % NZ, 1 - core), c)
    signal(at(y, z, 1 - core), c)
    for d in range(1, 4):
        signal(r, (c + d) % NX)

    load_rhs = pltpu.make_async_copy(rhs_hbm, rhs, loc.at[0])
    load_blk = pltpu.make_async_copy(blk_hbm, blk, loc.at[1])
    load_rhs.start()
    load_blk.start()

    k_row = jnp.broadcast_to(brow_ref[0, 0], (8, RHS))
    count = jnp.broadcast_to(count_ref[0], (8, RHS))
    valid = (count > 0) & (k_row * 128 + r > c)
    for i in range(2):
        wts[c, i] = jnp.where(valid & (k_row == i), F32(1.0), F32(0.0))

    need = 25 + jnp.where(c == 1, 2, jnp.where(c == 0, 1, 0)) - jnp.where(is_root, 1, 0)
    need = need + jnp.where(in_quarter & (r > 0), 1, 0)
    need = need + jnp.where(r == 0, jnp.where(c == 0, 15, 16), 0)
    need = need + jnp.where(is_c, 31, jnp.where(is_a, 32, jnp.where(is_root, 16, 0)))
    pl.semaphore_wait(barrier, need)

    for yy in range(NY):
        width = pl.ds(0, 128 * (yy + 1))

        @pl.when((y == yy) & in_quarter)
        def _():
            @pl.when(r > 0)
            def _():
                remote(diag_hbm.at[0, :, width], dq.at[r % 32, :, width], dsend.at[0], d0rec.at[yy % 2], 0, c).start()

            @pl.when(r == 0)
            def _():
                pltpu.make_async_copy(diag_hbm.at[0, :, width], dq.at[r % 32, :, width], d0rec.at[yy % 2]).start()

        later((y == yy) & in_quarter & (r > 0),
              remote(diag_hbm.at[0, :, width], dq.at[0, :, width], dsend.at[0], d0rec.at[0], 0, c))

    def send_diag(plane, k, slot):
        for yy in range(NY):
            width = pl.ds(0, 128 * (yy + 1))
            src = diag_hbm.at[k, :, width]

            @pl.when((y == yy) & (c == plane) & (r != k))
            def _():
                remote(src, dk.at[r, :, width], dsend.at[slot], drec.at[yy], k, plane).start()

            if yy == 0:
                @pl.when((c == plane) & (r == k))
                def _():
                    pltpu.make_async_copy(src, dk.at[r, :, width], drec.at[yy]).start()

            later((y == yy) & (c == plane) & (r != k),
                  remote(src, dk.at[0, :, width], dsend.at[slot], drec.at[0], 0, c))

    send_diag(0, 1, 1)

    for d in range(1, 4):
        remote(wts.at[c], wts.at[c], wsend.at[d - 1], wrec.at[c], r, (c + d) % NX).start()

    pair = (c == 3) & (r >= 4)
    lend = (c == 2) & (r == 3)
    lower = pl.ds(512, 512)

    @pl.when(pair | lend)
    def _():
        remote(blk_hbm, blk2, bsend, brec, r, 1).start()

    @pl.when((c == 1) & (r >= 4))
    def _():
        remote(blk_hbm.at[lower], blk2.at[lower], bsend, brec, r, 3).start()

    later(pair | lend, remote(blk_hbm, blk2, bsend, brec, r, 0))
    later((c == 1) & (r >= 4), remote(blk_hbm.at[lower], blk2.at[lower], bsend, brec, r, 0))

    for j in range(4):
        @pl.when(c != j)
        def _():
            pltpu.make_async_copy(wts.at[j], wts.at[j], wrec.at[j]).wait()

    send_diag(1, 2, 1)
    send_diag(1, 3, 2)
    load_rhs.wait()
    load_blk.wait()

    for d in range(3):
        later(None, remote(wts.at[0], wts.at[0], wsend.at[d], wrec.at[0], 0, c))

    def send_con(d):
        remote(con.at[c], con.at[c], xsend.at[d - 1], xrec.at[c], r, (c + d) % NX).start()

    def wait_con(j):
        pltpu.make_async_copy(con.at[j], con.at[j], xrec.at[j]).wait()

    def line(p):
        return (p % NZ) * 2 + p // NZ

    def squeeze(ref, block, width):
        part = ref[pl.ds(16 * block, 16), :, pl.ds(0, width)]
        return part.astype(F32).reshape(128, width).astype(BF16)

    def put_q(block, v):
        qn[pl.ds(2 * block, 2)] = v.astype(BF16).reshape(2, PIECE, RHS)

    for cc in range(NX):
        @pl.when((r == 0) & (c == cc))
        def _():
            piv[...] = rhs[0].astype(BF16)
            for h in range(2):
                block = 2 * cc + h
                width = 128 * (block + 1)
                sixteen = dq.at[pl.ds(16 * h, 16), :, pl.ds(0, width)]
                pltpu.make_async_copy(sixteen, sixteen, d0rec.at[h]).wait()
                put_q(block, jnp.dot(squeeze(dq, h, width), piv[pl.ds(0, width), :], preferred_element_type=F32))
            part = pl.ds(4 * cc, 4)
            for t in range(1, 4):
                remote(qn.at[part], qc.at[part], qsend.at[t - 1], qrec.at[cc], t, 0).start()
            for p in range(4 * cc, 4 * cc + 4):
                if p == 0:
                    pltpu.make_async_copy(qn.at[p], qb.at[0, p], prec.at[0]).start()
                else:
                    remote(qn.at[p], qb.at[0, p], p1send.at[0, p % 4], prec.at[0], line(p), 0).start()

    for p in range(4):
        later((r == 0) & ((c > 0) | (p > 0)), remote(qn.at[p], qb.at[0, p], p1send.at[0, p], prec.at[0], 0, 0))
    part0 = pl.ds(0, 4)
    later(r == 0, *[remote(qn.at[part0], qc.at[part0], qsend.at[t], qrec.at[0], 1, 0) for t in range(3)])

    @pl.when(is_root)
    def _():
        for block in range(8):
            width = 128 * (block + 1)
            sixteen = dk.at[pl.ds(16 * block, 16), :, pl.ds(0, width)]
            pltpu.make_async_copy(sixteen, sixteen, drec.at[block]).wait()
            dm[pl.ds(128 * block, 128), pl.ds(0, width)] = squeeze(dk, block, width)

    def times(a_ref, q_ref, g, put):
        b = q_ref[pl.ds(4 * g, 4)].reshape(256, RHS)

        def body(i, carry):
            at_rows = pl.ds(pl.multiple_of(i * 256, 256), 256)
            put(at_rows, jnp.dot(a_ref[at_rows, pl.ds(256 * g, 256)], b, preferred_element_type=F32))
            return carry

        lax.fori_loop(0, 4, body, 0)

    @pl.when(early)
    def _():
        for n, g in enumerate(ORDER):
            part = pl.ds(4 * g, 4)
            pltpu.make_async_copy(qc.at[part], qc.at[part], qrec.at[g]).wait()

            @pl.when(is_b)
            def _():
                remote(qc.at[part], qc.at[part], fsend.at[g], qrec.at[g], 3, 1).start()

            def put(at_rows, step):
                own[at_rows, :] = step if n == 0 else own[at_rows, :] + step

            times(blk, qc, g, put)

    @pl.when(is_a)
    def _():
        left[...] = rhs[0] - own[...]

    @pl.when(is_b | is_c)
    def _():
        wait_con(0)
        left[...] = rhs[0] - own[...] - con[0].astype(F32)

    @pl.when(is_c)
    def _():
        pltpu.make_async_copy(blk2, blk2, brec).wait()
        for g in ORDER:
            part = pl.ds(4 * g, 4)
            pltpu.make_async_copy(qc2.at[part], qc2.at[part], q2rec.at[g]).wait()

            def put(at_rows, step):
                left[at_rows, :] = left[at_rows, :] - step

            times(blk2, qc2, g, put)

    def scatter(p):
        slot = r // 2
        remote(qn.at[p], qb.at[slot, p], p1send.at[0, p], prec.at[slot], line(p), r).start()

        @pl.when(is_a)
        def _():
            remote(qn.at[p], qb.at[0, p], p1send.at[1, p], prec.at[0], line(p), 3).start()

        @pl.when(is_c)
        def _():
            if line(p) == 3:
                pltpu.make_async_copy(qn.at[p], qb.at[1, p], prec.at[1]).start()
            else:
                remote(qn.at[p], qb.at[1, p], p1send.at[1, p], prec.at[1], line(p), 1).start()

    @pl.when(is_root)
    def _():
        piv[...] = left[...].astype(BF16)
        for g in ORDER:
            for block in (2 * g, 2 * g + 1):
                width = 128 * (block + 1)
                put_q(block, jnp.dot(dm[pl.ds(128 * block, 128), pl.ds(0, width)], piv[pl.ds(0, width), :],
                                     preferred_element_type=F32))

                @pl.when(is_c)
                def _():
                    scatter(2 * block)
                    scatter(2 * block + 1)

            part = pl.ds(4 * g, 4)

            @pl.when(is_a)
            def _():
                remote(qn.at[part], qc.at[part], qsend.at[g], qrec.at[g], 2, 1).start()

            @pl.when(is_b)
            def _():
                remote(qn.at[part], qc2.at[part], qsend.at[g], q2rec.at[g], 3, 1).start()
                for p in range(4 * g, 4 * g + 4):
                    scatter(p)

    later(is_b, *[remote(qc.at[part0], qc.at[part0], fsend.at[g], qrec.at[0], 0, 0) for g in range(4)])
    later(is_a | is_b, *[remote(qn.at[part0], qc.at[part0], qsend.at[g], qrec.at[0], 0, 0) for g in range(4)])
    for p in range(16):
        later(is_root, remote(qn.at[p], qb.at[0, p], p1send.at[0, p], prec.at[0], 0, 3))
        later(is_a, remote(qn.at[p], qb.at[0, p], p1send.at[1, p], prec.at[0], 0, 3))
        if line(p) != 3:
            later(is_c, remote(qn.at[p], qb.at[0, p], p1send.at[1, p], prec.at[0], 0, 3))

    @pl.when(early)
    def _():
        con[c] = own[...].astype(BF16)

    @pl.when(support)
    def _():
        @pl.when(r == 3)
        def _():
            pl.semaphore_wait(turn, 1)

        send_con(1)

        @pl.when(r == 2)
        def _():
            remote(con.at[0], con.at[0], xsend.at[0], xrec.at[0], 0, c).wait_send()
            pl.semaphore_signal(turn, inc=1, device_id={"row": 3, "col": 0}, device_id_type=MESH)

    @pl.when(is_a)
    def _():
        for p in range(16):
            scatter(p)

    mine = core * 8 + z
    first = c < 2

    def gather(slot, active):
        @pl.when(active)
        def _():
            piece = qb.at[slot, mine]
            pltpu.make_async_copy(piece, piece, prec.at[slot]).wait()

            @pl.when(y == 0)
            def _():
                for d in (4, 3, 5, 2, 6, 1, 7):
                    remote(piece, piece, p2send.at[slot, d - 1], prec.at[slot], at(d, z, core), c).start()

            for d in (4, 3, 5, 2, 6, 1, 7):
                remote(piece, piece, p3send.at[slot, d - 1], p3rec.at[slot], at(y, (z + d) % NZ, core), c).start()
            seven = qb.at[slot, pl.ds(0, 7)]
            pltpu.make_async_copy(seven, seven, p3rec.at[slot]).wait()
            half = qb.at[slot, pl.ds(8 * core, 8)]
            remote(half, half, p4send.at[slot], p4rec.at[slot], at(y, z, 1 - core), c).start()
            other = qb.at[slot, pl.ds(8 * (1 - core), 8)]
            pltpu.make_async_copy(other, other, p4rec.at[slot]).wait()

        piece0 = qb.at[0, 0]
        half0 = qb.at[0, pl.ds(0, 8)]
        later(active & (y == 0), *[remote(piece0, piece0, p2send.at[slot, d], prec.at[slot], 0, c) for d in range(7)])
        later(active, *[remote(piece0, piece0, p3send.at[slot, d], p3rec.at[slot], 0, c) for d in range(7)])
        later(active, remote(half0, half0, p4send.at[slot], p4rec.at[slot], 0, c))

    def compute(k, a_ref, slot, t):
        at_rows = pl.ds(256 * t, 256)
        b = qb[slot].reshape(BS, RHS)
        con[k, at_rows, :] = jnp.dot(a_ref[at_rows, :], b, preferred_element_type=F32).astype(BF16)

    def tile_of(k, t):
        return con.at[k, pl.ds(256 * t, 256)]

    def share(k, plane, a_ref, slot, which, sends, recs):
        @pl.when((c == plane) & which)
        def _():
            h = plane // 2
            for t in (2 * h, 2 * h + 1):
                compute(k, a_ref, slot, t)
                for d in (1, 3):
                    remote(tile_of(k, t), tile_of(k, t), sends.at[d // 2, t % 2], recs.at[t], r, (c + d) % NX).start()
            for t in (2 - 2 * h, 3 - 2 * h):
                compute(k, a_ref, slot, t)

    gather(0, c != 2)
    low = r < 4
    high = r >= 4

    @pl.when(first & jnp.logical_not(early) & ((c == 0) | low))
    def _():
        for t in range(4):
            compute(c, blk, 0, t)

    for d in (1, 3, 2):
        @pl.when(first & ((c == 0) | low) & jnp.logical_not(support & (d == 1)))
        def _():
            send_con(d)

    whole = (c == 0) | (c == 2) | ((c == 1) & low)
    later(whole & ((c > 0) | (r != 2)), remote(con.at[0], con.at[0], xsend.at[0], xrec.at[0], 0, c))
    later(whole, *[remote(con.at[0], con.at[0], xsend.at[d], xrec.at[0], 0, c) for d in (1, 2)])
    def give(t, d):
        remote(tile_of(1, t), tile_of(1, t), h1send.at[d - 1, t % 2], h1rec.at[t], r, (c + d) % NX).start()

    @pl.when((c == 1) & high)
    def _():
        for t in (0, 1):
            compute(1, blk, 0, t)
            for d in (2, 1, 3):
                give(t, d)
        for t in (2, 3):
            compute(1, blk, 0, t)

    @pl.when((c == 3) & high)
    def _():
        pltpu.make_async_copy(blk2.at[lower], blk2.at[lower], brec).wait()
        for t in (2, 3):
            compute(1, blk2, 0, t)
            for d in (1, 3):
                give(t, d)

    tile0 = tile_of(1, 0)
    later((c % 2 == 1) & high, *[remote(tile0, tile0, h1send.at[d, t], h1rec.at[0], r, 0) for d in (0, 2) for t in range(2)])
    later((c == 1) & high, *[remote(tile0, tile0, h1send.at[1, t], h1rec.at[0], r, 0) for t in range(2)])

    @pl.when(first)
    def _():
        solved_ref[...] = qb[0].astype(F32).reshape(BS, RHS)

    gather(1, c > 0)

    @pl.when(c == 2)
    def _():
        for t in range(4):
            compute(2, blk, 1, t)

    @pl.when(c == 2)
    def _():
        for d in (2, 1, 3):
            send_con(d)

    @pl.when((c == 1) & (r >= 4))
    def _():
        pltpu.make_async_copy(blk2, blk2, brec).wait()

    @pl.when((c == 1) & (r < 4))
    def _():
        con[3] = jnp.zeros((BS, RHS), BF16)

    share(3, 1, blk2, 1, high, hsend, hrec)

    @pl.when((c == 1) & low)
    def _():
        for t in (0, 1):
            for d in (1, 3):
                remote(tile_of(3, t), tile_of(3, t), hsend.at[d // 2, t], hrec.at[t], r, (c + d) % NX).start()

    share(3, 3, blk, 1, c == 3, hsend, hrec)
    later(c % 2 == 1, *[remote(tile_of(3, 0), tile_of(3, 0), hsend.at[d, t], hrec.at[0], r, 0) for d in range(2) for t in range(2)])

    @pl.when(c >= 2)
    def _():
        solved_ref[...] = qb[1].astype(F32).reshape(BS, RHS)

    def update(j, base, rows):
        got = con[j, rows, :].astype(F32).reshape(rows.size // 8, 8, RHS)
        for i in range(2):
            step = (got * wts[j, i][None]).reshape(rows.size, RHS)
            rem_ref[i, rows, :] = base[i, rows, :] - step

    for j in range(3):
        waits = (c != j) & jnp.logical_not((is_b | is_c) & (j == 0))

        @pl.when(waits & (low if j == 1 else c >= 0))
        def _():
            wait_con(j)

        if j == 1:
            for t in range(4):
                @pl.when((c != 1 if t < 2 else c % 2 == 0) & high)
                def _():
                    pltpu.make_async_copy(tile_of(1, t), tile_of(1, t), h1rec.at[t]).wait()

        update(j, rhs if j == 0 else rem_ref, pl.ds(0, BS))

    for n, t in enumerate((0, 2, 1, 3)):
        @pl.when(c % 2 == 0)
        def _():
            pltpu.make_async_copy(tile_of(3, t), tile_of(3, t), hrec.at[t]).wait()

        update(3, rem_ref, pl.ds(256 * t, 256))

    finish()


def hand_over(solved_in, rem_in, solved_out, rem_out, sems):
    pairs = [(rem_in.at[0], rem_out.at[0, 0]), (rem_in.at[1], rem_out.at[1, 0]), (solved_in, solved_out.at[0, 0])]
    moves = []
    for n, (src, dst) in enumerate(pairs):
        for t in range(4):
            rows = pl.ds(256 * t, 256)
            moves.append(pltpu.make_async_copy(src.at[rows], dst.at[rows], sems.at[n, t]))
    for move in moves:
        move.start()
    for move in moves:
        move.wait()


def on_device(rhs, diag_inv, blocks, block_rows, counts):
    vmem = pl.BlockSpec(memory_space=pltpu.VMEM)
    hbm = pl.BlockSpec(memory_space=pltpu.HBM)
    dma = pltpu.SemaphoreType.DMA
    here = pltpu.with_memory_space_constraint
    solved, rem = pl.pallas_call(
        kernel,
        out_shape=(pltpu.VMEM((BS, RHS), F32), pltpu.VMEM((2, BS, RHS), F32)),
        in_specs=[vmem, vmem, hbm, hbm, hbm],
        out_specs=(vmem, vmem),
        scratch_shapes=[
            pltpu.VMEM((2, BS, RHS), F32),
            pltpu.VMEM((BS, BS), BF16),
            pltpu.VMEM((BS, BS), BF16),
            pltpu.VMEM((32, 8, BS), BF16),
            pltpu.VMEM((128, 8, BS), BF16),
            pltpu.VMEM((BS, BS), BF16),
            pltpu.VMEM((BS, RHS), F32),
            pltpu.VMEM((BS, RHS), F32),
            pltpu.VMEM((BS, RHS), BF16),
            pltpu.VMEM((16, PIECE, RHS), BF16),
            pltpu.VMEM((16, PIECE, RHS), BF16),
            pltpu.VMEM((16, PIECE, RHS), BF16),
            pltpu.VMEM((2, 16, PIECE, RHS), BF16),
            pltpu.VMEM((4, BS, RHS), BF16),
            pltpu.VMEM((4, 2, 8, RHS), F32),
            dma((2,)), dma((3,)), dma((2,)), dma((8,)), dma((4,)), dma((4,)), dma((4,)), dma((4,)),
            dma((2, 16)), dma((2,)), dma((2, 7)), dma((2, 7)), dma((2,)), dma((2,)), dma((2,)),
            dma((3,)), dma((4,)), dma((3, 2)), dma((4,)), dma((2, 2)), dma((4,)), dma((3,)), dma((4,)), dma, dma, pltpu.SemaphoreType.REGULAR,
        ],
        compiler_params=pltpu.CompilerParams(
            collective_id=0, has_side_effects=True, vmem_limit_bytes=40 << 20
        ),
    )(
        block_rows, counts, here(rhs.reshape(2, BS, RHS), pltpu.HBM), here(diag_inv, pltpu.HBM),
        here(blocks.reshape(BS, BS), pltpu.HBM),
    )
    return pl.pallas_call(
        hand_over,
        out_shape=(
            jax.ShapeDtypeStruct((1, 1, BS, RHS), F32),
            jax.ShapeDtypeStruct((2, 1, BS, RHS), F32),
        ),
        in_specs=[vmem, vmem],
        out_specs=(hbm, hbm),
        scratch_shapes=[dma((3, 4))],
        compiler_params=pltpu.CompilerParams(vmem_limit_bytes=4 << 20),
    )(here(solved, pltpu.VMEM), here(rem, pltpu.VMEM))


def solution(mesh):
    in_specs = (
        P(None, "row", None, None),
        P(None, "row", None),
        P(None, "col", "row", None, None, None),
        P(None, "col", "row", None),
        P(None, "col", "row"),
    )
    out_specs = (P(None, "col", None, None), P(None, "row", None, None))
    return jax.shard_map(
        on_device, mesh=mesh, in_specs=in_specs, out_specs=out_specs, check_vma=False
    )
```
